256 devices in a mesh: group: 4 (over y), seq: 16 (over z, x_hi), mp: 4 (over x_lo, core).
Axes of the slice: x: 4 (x_hi: 2, x_lo: 2; x = x_hi * 2 + x_lo), y: 4, z: 8, core: 2. Of those that a mesh axis runs over, the one named last changes fastest.
Arguments:
- gen_input: bfloat16 [4096, 5120], P('seq'), may hold values from -22 to 22
- noise: bfloat16 [4096, 5120], P('seq'), may hold values from -22 to 22
- gen_steps: int32 [2], replicated, may hold values from 0 to 15
- critic_steps: int32 [2], replicated, may hold values from 0 to 15
- row_order: int32 [16, 256], P('seq'), may hold values from 0 to 255, each once within a row
- gen_wq: bfloat16 [5120, 2560], P('seq', 'mp'), may hold values from -0.078125 to 0.078125
- gen_wo: bfloat16 [5120, 2560], P('seq', 'mp'), may hold values from -0.125 to 0.125
- teacher_wq: bfloat16 [5120, 2560], P('seq', 'mp'), may hold values from -0.078125 to 0.078125
- teacher_wo: bfloat16 [5120, 2560], P('seq', 'mp'), may hold values from -0.125 to 0.125
- fake_wq: bfloat16 [5120, 2560], P('seq', 'mp'), may hold values from -0.078125 to 0.078125
- fake_wo: bfloat16 [5120, 2560], P('seq', 'mp'), may hold values from -0.125 to 0.125
- gen_mod: bfloat16 [16, 3, 5120], replicated, may hold values from -4 to 4
- teacher_mod: bfloat16 [16, 3, 5120], replicated, may hold values from -4 to 4
- fake_mod: bfloat16 [16, 3, 5120], replicated, may hold values from -4 to 4
- text_keys: bfloat16 [4, 512, 2560], P('group', None, 'mp'), may hold values from -6 to 6
- text_values: bfloat16 [4, 512, 2560], P('group', None, 'mp'), may hold values from -24 to 24
Outputs:
- predictions: bfloat16 [4, 4096, 5120], P('group', 'seq', 'mp')
- input_grads: float32 [4, 4096, 5120], P('group', 'seq', 'mp')
The draws below stay inside these ranges and needn't reach their ends.
Inputs may be any that keep to these rules, and one draw needn't show every extreme that they name: `row_order`: each row lists the 256 positions of one block once each.
All inputs are finite; a program needn't handle non-finite values. Where the reference program divides by a largest or mean magnitude, that divisor is 1e-20 or more.
Results may differ from the reference program's by a relative error of at most 0.038.
Values may be sent and summed in bfloat16 or wider, within the bound.
A program may use at most 128 MiB of HBM per device.

```python
import math
import jax
import jax.numpy as jnp
from jax import lax

D = 5120
HEAD = 128
TEXT = 512
T_STEPS = 16
SAMPLES = 2
GROUPS = 4
TOK_DEV = 256
HD = 2560
TOKENS = 4096
N_SEQ = 16
N_MP = 4


def column_spread(key):
    column = jnp.arange(D, dtype=jnp.float32) / (D - 1)
    return 10.0 ** (jax.random.uniform(key, (D,), dtype=jnp.float32) - 0.5) * 3.0 ** (column - 0.5)


def draw_gen_input(key, part):
    key = jax.random.fold_in(key, 11)
    first, second = jax.random.split(key)
    spread = column_spread(first)
    base = jnp.clip(jax.random.normal(second, (TOKENS, D), jnp.float32), -4.0, 4.0)
    return jnp.clip(base * spread[None, :], -22.0, 22.0).astype(jnp.bfloat16)


def draw_noise(key, part):
    key = jax.random.fold_in(key, 23)
    first, second = jax.random.split(key)
    spread = column_spread(first)
    position = jnp.arange(TOKENS, dtype=jnp.float32) / (TOKENS - 1)
    ramp = 3.0 ** (position - 0.5)
    base = jnp.clip(jax.random.normal(second, (TOKENS, D), jnp.float32), -4.0, 4.0)
    return jnp.clip(base * ramp[:, None] * spread[None, :], -22.0, 22.0).astype(jnp.bfloat16)


def block_levels(stream_key, dims, pieces, low, high):
    def one(dim, blocks):
        draws = jax.random.uniform(jax.random.fold_in(jax.random.fold_in(stream_key, 6), dim), (blocks,), jnp.float32, low / len(pieces), high / len(pieces))
        return jnp.repeat(jnp.exp(draws), dims[dim] // blocks).reshape((-1,) + (1,) * (len(dims) - dim - 1))

    factor_of = one(*pieces[0])
    for cut in pieces[1:]:
        factor_of = factor_of * one(*cut)
    return factor_of


def centred(stream_key, extent, scale, bound, pieces=(), held_as=jnp.bfloat16):
    values = scale * jax.random.normal(stream_key, extent, jnp.float32)
    if pieces:
        values = values * block_levels(stream_key, extent, pieces, -0.22, 0.18)
    return jnp.clip(values, -bound, bound).astype(held_as)


def setup_inputs(seed: int = 0) -> dict:
    streams_of = jax.random.split(jax.random.key(seed), 17)
    gen_input = draw_gen_input(jax.random.fold_in(streams_of[16], 71), 0)
    noise = draw_noise(jax.random.fold_in(streams_of[16], 71), 0)
    gen_steps = jax.random.randint(streams_of[2], (SAMPLES,), 0, T_STEPS).astype(jnp.int32)
    critic_steps = jax.random.randint(streams_of[3], (SAMPLES,), 0, T_STEPS).astype(jnp.int32)
    row_order = jax.vmap(lambda own: jax.random.permutation(own, TOK_DEV))(jax.random.split(streams_of[4], N_SEQ)).reshape((N_SEQ, TOK_DEV)).astype(jnp.int32)
    gen_wq = centred(streams_of[5], (D, HD), D ** -0.5, 0.078125, ((0, 16), (1, 4)))
    gen_wo = centred(streams_of[6], (D, HD), HD ** -0.5, 0.125, ((0, 16), (1, 4)))
    teacher_wq = centred(streams_of[7], (D, HD), D ** -0.5, 0.078125, ((0, 16), (1, 4)))
    teacher_wo = centred(streams_of[8], (D, HD), HD ** -0.5, 0.125, ((0, 16), (1, 4)))
    fake_wq = centred(streams_of[9], (D, HD), D ** -0.5, 0.078125, ((0, 16), (1, 4)))
    fake_wo = centred(streams_of[10], (D, HD), HD ** -0.5, 0.125, ((0, 16), (1, 4)))
    gen_mod = centred(streams_of[11], (T_STEPS, 3, D), 0.8, 4.0)
    teacher_mod = centred(streams_of[12], (T_STEPS, 3, D), 0.8, 4.0)
    fake_mod = centred(streams_of[13], (T_STEPS, 3, D), 0.8, 4.0)
    text_keys = centred(streams_of[14], (GROUPS, TEXT, HD), 1.0, 6.0, ((0, 4), (2, 4)))
    text_values = centred(streams_of[15], (GROUPS, TEXT, HD), 4.0, 24.0, ((0, 4), (2, 4)))
    return dict(gen_input=gen_input, noise=noise, gen_steps=gen_steps, critic_steps=critic_steps, row_order=row_order, gen_wq=gen_wq, gen_wo=gen_wo, teacher_wq=teacher_wq, teacher_wo=teacher_wo, fake_wq=fake_wq, fake_wo=fake_wo, gen_mod=gen_mod, teacher_mod=teacher_mod, fake_mod=fake_mod, text_keys=text_keys, text_values=text_values)


EPSILON = 1e-06
FLOOR_EPSILON = 1e-05
GUIDANCE = 3.0

def head_norm(values):
    shaped = values.reshape(values.shape[0], -1, HEAD)
    factor = lax.rsqrt(lax.optimization_barrier(jnp.mean(shaped * shaped, axis=2, keepdims=True)) + EPSILON)
    return (shaped, factor)

def normed_keys_of(key_cache):
    shaped, factor = head_norm(key_cache.astype(jnp.float32))
    return (shaped * factor).astype(jnp.bfloat16).reshape(key_cache.shape)

def attend(query_rows, keys_normed, value_cache):
    query_heads, query_scale = head_norm(query_rows)
    normed = (query_heads * query_scale).astype(jnp.bfloat16)
    key_heads = keys_normed.reshape(keys_normed.shape[0], -1, HEAD)
    value_heads = value_cache.reshape(value_cache.shape[0], -1, HEAD)
    scores = jnp.einsum('nhd,thd->hnt', normed.astype(jnp.float32), key_heads.astype(jnp.float32)) * HEAD ** (-0.5)
    exponent = jnp.exp(scores)
    softmax_rows = (exponent / lax.optimization_barrier(jnp.sum(exponent, axis=2, keepdims=True))).astype(jnp.bfloat16)
    mixed_rows = jnp.einsum('hnt,thd->nhd', softmax_rows.astype(jnp.float32), value_heads.astype(jnp.float32))
    return (mixed_rows.reshape(query_rows.shape[0], -1).astype(jnp.bfloat16), softmax_rows, query_heads, query_scale)

def attend_back(query_rows, grad_mixed, keys_normed, value_cache):
    unused, softmax_rows, query_heads, query_scale = attend(query_rows, keys_normed, value_cache)
    count = grad_mixed.shape[0]
    key_heads = keys_normed.reshape(keys_normed.shape[0], -1, HEAD).astype(jnp.float32)
    value_heads = value_cache.reshape(value_cache.shape[0], -1, HEAD).astype(jnp.float32)
    grad_heads = grad_mixed.reshape(count, -1, HEAD).astype(jnp.float32)
    grad_probs = jnp.einsum('nhd,thd->hnt', grad_heads, value_heads)
    weights = softmax_rows.astype(jnp.float32)
    grad_scores = (weights * (grad_probs - lax.optimization_barrier(jnp.sum(weights * grad_probs, axis=2, keepdims=True)))).astype(jnp.bfloat16)
    grad_normed = jnp.einsum('hnt,thd->nhd', grad_scores.astype(jnp.float32), key_heads) * HEAD ** (-0.5)
    unit = query_heads * query_scale
    grad_query = query_scale * (grad_normed - unit * lax.optimization_barrier(jnp.mean(unit * grad_normed, axis=2, keepdims=True)))
    return grad_query.reshape(count, -1).astype(jnp.bfloat16)

def in_blocks(function, arrays):
    count = arrays[0].shape[0]
    size = math.gcd(count, 512)
    shaped = tuple((item.reshape((count // size, size) + item.shape[1:]) for item in arrays))
    result = lax.map(lambda block: function(*block), shaped)
    return result.reshape((count,) + result.shape[2:])

def grouped_sum(left, right_t):
    width = left.shape[1] // N_MP
    total = jnp.zeros((left.shape[0], right_t.shape[0]), jnp.float32)
    for number in range(N_MP):
        piece = jnp.dot(left[:, number * width:(number + 1) * width], right_t[:, number * width:(number + 1) * width].T, preferred_element_type=jnp.float32)
        rounded = lax.optimization_barrier(piece.astype(jnp.bfloat16))
        total = total + rounded.astype(jnp.float32)
    return total

def forward(rows, modulation, weight_q, weight_o, keys_normed, value_cache):
    shift, scale, gate = modulation
    rows_float = rows.astype(jnp.float32)
    inverse = lax.rsqrt(lax.optimization_barrier(jnp.mean(rows_float * rows_float, axis=2, keepdims=True)) + EPSILON)
    hidden = (rows_float * inverse * (1.0 + scale) + shift).astype(jnp.bfloat16).reshape(-1, D)
    query_rows = jnp.dot(hidden, weight_q, preferred_element_type=jnp.float32)
    mixed_rows = in_blocks(lambda block: attend(block, keys_normed, value_cache)[0], (query_rows,))
    branch = grouped_sum(mixed_rows, weight_o).reshape(rows.shape)
    output = (rows_float + gate * branch).astype(jnp.bfloat16)
    return (output, (rows_float, inverse, query_rows))

def backward(modulation, weight_q, weight_o, keys_normed, value_cache, saved, cotangent):
    shift, scale, gate = modulation
    rows_float, inverse, query_rows = saved
    grad_out = (gate * cotangent).astype(jnp.bfloat16).reshape(-1, D)
    grad_mixed = jnp.dot(grad_out, weight_o, preferred_element_type=jnp.float32).astype(jnp.bfloat16)
    grad_query = in_blocks(lambda qblock, gblock: attend_back(qblock, gblock, keys_normed, value_cache), (query_rows, grad_mixed))
    grad_hidden = grouped_sum(grad_query, weight_q).reshape(rows_float.shape)
    multiplier = 1.0 + scale
    inner = lax.optimization_barrier(jnp.mean(rows_float * multiplier * grad_hidden, axis=2, keepdims=True))
    return cotangent + inverse * multiplier * grad_hidden - rows_float * inverse ** 3 * inner

def table_rows(mod_table, steps):
    chosen = mod_table.astype(jnp.float32)[steps]
    return (chosen[:, 0][:, None, :], chosen[:, 1][:, None, :], chosen[:, 2][:, None, :])

def reference(gen_input, noise, gen_steps, critic_steps, row_order, gen_wq, gen_wo, teacher_wq, teacher_wo, fake_wq, fake_wo, gen_mod, teacher_mod, fake_mod, text_keys, text_values):
    keys_normed = [normed_keys_of(text_keys[number]) for number in range(GROUPS)]
    gen_rows = gen_input.reshape(SAMPLES, -1, D)
    gen_modulation = table_rows(gen_mod, gen_steps)
    generated, gen_saved = forward(gen_rows, gen_modulation, gen_wq, gen_wo, keys_normed[0], text_values[0])
    blocks = generated.reshape(N_SEQ, TOK_DEV, D)
    arranged = jax.vmap(lambda block, indices: jnp.take(block, indices, axis=0))(blocks, row_order).reshape(SAMPLES, -1, D)
    angle = 0.5 * jnp.pi * (critic_steps.astype(jnp.float32) + 1.0) / (T_STEPS + 1.0)
    alpha = jnp.cos(angle)[:, None, None]
    sigma = jnp.sin(angle)[:, None, None]
    noised = (alpha * arranged.astype(jnp.float32) + sigma * noise.reshape(SAMPLES, -1, D).astype(jnp.float32)).astype(jnp.bfloat16)
    teacher_modulation = table_rows(teacher_mod, critic_steps)
    fake_modulation = table_rows(fake_mod, critic_steps)
    cond, cond_saved = forward(noised, teacher_modulation, teacher_wq, teacher_wo, keys_normed[1], text_values[1])
    uncond, uncond_saved = forward(noised, teacher_modulation, teacher_wq, teacher_wo, keys_normed[2], text_values[2])
    faked, fake_saved = forward(noised, fake_modulation, fake_wq, fake_wo, keys_normed[3], text_values[3])
    real = GUIDANCE * cond.astype(jnp.float32) - (GUIDANCE - 1.0) * uncond.astype(jnp.float32)
    arranged_float = arranged.astype(jnp.float32)
    denominator = lax.optimization_barrier(jnp.mean(jnp.abs(arranged_float - real), axis=(1, 2), keepdims=True)) + FLOOR_EPSILON
    score = (faked.astype(jnp.float32) - real) / denominator
    score_blocks = score.reshape(N_SEQ, TOK_DEV, D)
    gen_cotangent = jax.vmap(lambda values, indices: jnp.zeros_like(values).at[indices].set(values))(score_blocks, row_order).reshape(SAMPLES, -1, D)
    grad_gen = backward(gen_modulation, gen_wq, gen_wo, keys_normed[0], text_values[0], gen_saved, gen_cotangent)
    grad_cond = backward(teacher_modulation, teacher_wq, teacher_wo, keys_normed[1], text_values[1], cond_saved, -GUIDANCE * score)
    grad_uncond = backward(teacher_modulation, teacher_wq, teacher_wo, keys_normed[2], text_values[2], uncond_saved, (GUIDANCE - 1.0) * score)
    grad_fake = backward(fake_modulation, fake_wq, fake_wo, keys_normed[3], text_values[3], fake_saved, faked.astype(jnp.float32) - arranged_float)
    predictions = jnp.stack([generated.reshape(TOKENS, D), cond.reshape(TOKENS, D), uncond.reshape(TOKENS, D), faked.reshape(TOKENS, D)])
    input_grads = jnp.stack([grad_gen.reshape(TOKENS, D), grad_cond.reshape(TOKENS, D), grad_uncond.reshape(TOKENS, D), grad_fake.reshape(TOKENS, D)])
    return (predictions, input_grads)
```

```python
import jax
import jax.numpy as jnp
from jax import lax
from jax.experimental import pallas as pl
from jax.experimental.pallas import tpu as pltpu
from jax.sharding import PartitionSpec as P

D = 5120
HEAD = 128
SAMPLES = 2
GROUPS = 4
TOK = 256
TEXT = 512
COLS = 640
HEADS = 5
SUB = 80
SLICE = 320
QUARTER = 1280
QROWS = TOK + 16
QCOLS = COLS + 128
LAG = 3
EPSILON = 1e-06
FLOOR_EPSILON = 1e-05
GUIDANCE = 3.0
BF = jnp.bfloat16
F32 = jnp.float32

GQ, GO, TQ, FQ, TO, FO = range(6)


def dot_nn(a, b):
    return lax.dot_general(a, b, (((1,), (0,)), ((), ())), preferred_element_type=F32)


def dot_nt(a, b):
    return lax.dot_general(a, b, (((1,), (1,)), ((), ())), preferred_element_type=F32)


def dot_tn(a, b):
    return lax.dot_general(a, b, (((0,), (0,)), ((), ())), preferred_element_type=F32)


class Slots:
    def __init__(self):
        self.count = 0

    def take(self, number):
        first = self.count
        self.count += number
        return first


SLOTS = Slots()
RING = SLOTS.take(2 * 6 * 7)
XCH = SLOTS.take(6)
YQG = SLOTS.take(4)
YQC = SLOTS.take(4)
YMG = SLOTS.take(4)
YMC = SLOTS.take(4)
YPR = SLOTS.take(4)
YGN = SLOTS.take(4)
YNO = SLOTS.take(4)
YCO = SLOTS.take(4)
YGM = SLOTS.take(4)
YGQ = SLOTS.take(4)
YGH = SLOTS.take(4)
YDI = SLOTS.take(4)
RSC = SLOTS.take(8 * 2)
RSX = SLOTS.take(8)
AGM = SLOTS.take(4 * 3)
BUT = SLOTS.take(5)
INN = SLOTS.take(2)
N_SEM = SLOTS.count


def kernel(
    wown, a1, x1s, nzs, onehot, shifts, cols, scols, r1, keys, values,
    out4, ss_out, inner_out, dist_out,
    W, qsg, qsc, qbuf, qA, qq, probs, mb, PP, CC, SS, XX, G, an,
    send_p, send_c, send_h, gms, gmb, gq, isend, irecv, dsend, drecv,
    ssem, rsem,
):
    g = lax.axis_index("group")
    s = lax.axis_index("seq")
    m = lax.axis_index("mp")
    z, xh = s // 2, lax.rem(s, 2)
    xl, c = m // 2, lax.rem(m, 2)
    m_core = 2 * xl + 1 - c
    m_x = 2 * (1 - xl) + c
    s_x = 2 * z + 1 - xh
    z_pair = z + 1 - 2 * lax.rem(z, 2)
    z_far = z + 2 - 4 * lax.rem(z // 2, 2)
    s_up = lax.rem(z + 1, 8) * 2 + xh
    s_down = lax.rem(z + 7, 8) * 2 + xh
    s_pair = z_pair * 2 + xh
    s_far = z_far * 2 + xh
    others = [lax.rem(g + k, GROUPS) for k in (1, 2, 3)]
    pending = []

    def rdma(src, dst, send, recv, **where):
        return pltpu.make_async_remote_copy(
            src_ref=src, dst_ref=dst, send_sem=ssem.at[send], recv_sem=rsem.at[recv],
            device_id=where, device_id_type=pl.DeviceIdType.MESH,
        )

    def start(copy):
        copy.start()
        pending.append(copy)

    barrier = pltpu.get_barrier_semaphore()
    peers = [{"group": o} for o in others]
    peers += [{"mp": m_core}, {"mp": m_x}, {"seq": s_x}, {"seq": s_up}, {"seq": s_down}, {"seq": s_far}]
    for peer in peers:
        pl.semaphore_signal(barrier, inc=1, device_id=peer, device_id_type=pl.DeviceIdType.MESH)
    pl.semaphore_wait(barrier, len(peers))

    def rows_of(zz, x):
        return pl.ds(pl.multiple_of((lax.rem(zz + 16, 8) * 2 + x) * SUB, 16), SUB)

    def ring_copy(way, k, t):
        sem = RING + (way * 6 + k) * 7 + t
        if way == 0:
            rows = rows_of(z - t, xh)
            src = wown.at[k] if t == 0 else W.at[k, rows]
            return rdma(src, W.at[k, rows], sem, sem, seq=s_up)
        rows = rows_of(z + t, 1 - xh)
        return rdma(W.at[k, rows], W.at[k, rows], sem, sem, seq=s_down)

    def ring_wait(way, k, t):
        sem = RING + (way * 6 + k) * 7 + t
        rows = rows_of(z - 1 - t, xh) if way == 0 else rows_of(z + 1 + t, 1 - xh)
        rdma(W.at[k, rows], W.at[k, rows], sem, sem, seq=s_up).wait_recv()

    my_rows = rows_of(z, xh)
    for k in range(6):
        start(rdma(wown.at[k], W.at[k, my_rows], XCH + k, XCH + k, seq=s_x))
    for k in range(6):
        W[k, my_rows, :] = wown[k]

    state = {"tick": 0}

    def ring_to(last):
        while state["tick"] <= last:
            tick = state["tick"]
            for k in range(6):
                t = tick - LAG * k
                if t == 0:
                    start(ring_copy(0, k, 0))
                    other = rows_of(z, 1 - xh)
                    rdma(W.at[k, other], W.at[k, other], XCH + k, XCH + k, seq=s_x).wait_recv()
                    start(ring_copy(1, k, 0))
            for k in range(6):
                t = tick - LAG * k
                if 0 <= t <= 6:
                    for way in (0, 1):
                        ring_wait(way, k, t)
                        if t < 6:
                            start(ring_copy(way, k, t + 1))
            state["tick"] += 1

    def have(k):
        ring_to(LAG * k + 6)

    def y_send(base, dg, src, dst):
        start(rdma(src, dst, base + dg, base + g, group=others[dg - 1]))

    def y_wait(base, source, ref):
        rdma(ref, ref, base, base + source, group=others[0]).wait_recv()

    def slice_rows(index):
        return pl.ds(pl.multiple_of(index * SLICE, 16), SLICE)

    def rs_first(r):
        for far in (1, 0):
            x = 1 - xl if far else xl
            start(rdma(PP.at[r, slice_rows(2 * x + 1 - c)], CC.at[r, x],
                       RSC + 2 * r + far, RSC + 2 * r + x, mp=m_core))

    def rs_core_wait(r, x):
        rdma(CC.at[r, x], CC.at[r, x], RSC + 2 * r, RSC + 2 * r + x, mp=m_core).wait_recv()

    def rs_second(r):
        rs_core_wait(r, 1 - xl)
        SS[r] = (PP[r, slice_rows(2 * (1 - xl) + c), :].astype(F32) + CC[r, 1 - xl].astype(F32)).astype(BF)
        start(rdma(SS.at[r], XX.at[r], RSX + r, RSX + r, mp=m_x))

    def rs_total(r):
        rs_core_wait(r, xl)
        rdma(XX.at[r], XX.at[r], RSX + r, RSX + r, mp=m_x).wait_recv()
        return (PP[r, slice_rows(m), :].astype(F32) + CC[r, xl].astype(F32)) + XX[r].astype(F32)

    def ag_first(r):
        rows = slice_rows(m)
        start(rdma(G.at[r, rows], G.at[r, rows], AGM + 3 * r, AGM + 3 * r, mp=m_x))
        start(rdma(G.at[r, rows], G.at[r, rows], AGM + 3 * r + 1, AGM + 3 * r + 1, mp=m_core))

    def ag_second(r):
        rows = slice_rows(m_x)
        rdma(G.at[r, rows], G.at[r, rows], AGM + 3 * r, AGM + 3 * r, mp=m_x).wait_recv()
        start(rdma(G.at[r, rows], G.at[r, rows], AGM + 3 * r + 2, AGM + 3 * r + 2, mp=m_core))

    def ag_wait(r):
        for extra, index in ((1, m_core), (2, 2 * (1 - xl) + 1 - c)):
            rows = slice_rows(index)
            rdma(G.at[r, rows], G.at[r, rows], AGM + 3 * r + extra, AGM + 3 * r + extra, mp=m_core).wait_recv()

    def planes(r, k, ref):
        def body(i, carry):
            rows = slice_rows(i)
            PP[r, rows, :] = dot_nt(W[k, rows, :], ref[...]).astype(BF)
            return carry
        lax.fori_loop(0, 4, body, 0)

    scaling = HEAD ** -0.5

    def lanes_of(h):
        return pl.ds(pl.multiple_of(h * HEAD, HEAD), HEAD)

    def attend(r, total, bias):
        qA[...] = total
        qq[...] = r * total + bias

        def head(h, carry):
            lanes = lanes_of(h)
            qh = qq[:, lanes]
            rq = lax.rsqrt(jnp.mean(qh * qh, axis=1, keepdims=True) + EPSILON)
            e = jnp.exp(dot_nt((qh * rq).astype(BF), keys[:, lanes]) * scaling)
            p = (e * (1.0 / jnp.sum(e, axis=1, keepdims=True))).astype(BF)
            probs[h] = p
            mb[g, :, lanes] = dot_nn(p, values[:, lanes]).astype(BF)
            return carry

        lax.fori_loop(0, HEADS, head, 0)

    def gathered(own):
        parts = [own] + [qbuf.at[o] for o in others]
        total = sum(p[0:TOK, 0:COLS].astype(F32) for p in parts)
        bias = sum(p[TOK:QROWS, 0:COLS].astype(F32) for p in parts)[0:1, :]
        extra = sum(p[0:TOK, COLS:QCOLS].astype(F32) for p in parts)
        return total, bias, extra

    def to_bf_rows(ref, part, bias, extra):
        ref[0:TOK, 0:COLS] = part.astype(BF)
        ref[TOK:QROWS, 0:COLS] = bias.astype(BF)
        ref[0:TOK, COLS:QCOLS] = extra
        ref[TOK:QROWS, COLS:QCOLS] = jnp.zeros((16, 128), BF)

    have(GQ)
    to_bf_rows(qsg, dot_tn(a1[...], W[GQ]), dot_nn(shifts[0], W[GQ]), jnp.zeros((TOK, 128), BF))
    gen_q = rdma(qsg, qbuf.at[g], YQG, YQG + g, group=0)

    @pl.when(g != 0)
    def _():
        gen_q.start()

    have(GO)

    gen_m = [rdma(mb.at[0], mb.at[0], YMG + k, YMG, group=others[k - 1]) for k in (1, 2, 3)]

    @pl.when(g == 0)
    def _():
        for o in others:
            y_wait(YQG, o, qbuf.at[o])
        total, bias, _ = gathered(qsg)
        attend(r1[...], total, bias)
        for copy in (gen_m[1], gen_m[0], gen_m[2]):
            copy.start()

    ring_to(LAG * TQ + 6)

    @pl.when(g != 0)
    def _():
        y_wait(YMG, 0, mb.at[0])

    planes(0, GO, mb.at[0])
    rs_first(0)
    rs_second(0)
    total = rs_total(0)
    gate_g, gate_t, gate_f = scols[:, 0:1], scols[:, 1:2], scols[:, 2:3]
    alpha, sigma = scols[:, 3:4], scols[:, 4:5]
    gen_s = (x1s[...].astype(F32) + gate_g * total).astype(BF)
    send_p[0] = gen_s
    arr = dot_nn(gen_s, onehot[...])
    noised = (alpha * arr + sigma * nzs[...].astype(F32)).astype(BF)
    G[0, slice_rows(m), :] = noised
    ag_first(0)
    ag_second(0)
    ag_wait(0)

    nf = G[0].astype(F32)
    sq = (nf * nf).astype(BF)
    squares = dot_tn(sq, jnp.ones((QUARTER, 128), BF))
    high = squares.astype(BF)
    low = (squares - high.astype(F32)).astype(BF)
    lane = lax.broadcasted_iota(jnp.int32, (TOK, 128), 1)
    extra = jnp.where(lane < 64, high.astype(F32), low.astype(F32)).astype(BF)
    an[0] = (nf * cols[:, 0:1]).astype(BF)
    an[1] = (nf * cols[:, 1:2]).astype(BF)
    have(TQ)
    to_bf_rows(qsc.at[0], dot_tn(an[0], W[TQ]), dot_nn(shifts[1], W[TQ]), extra)
    have(FQ)
    to_bf_rows(qsc.at[1], dot_tn(an[1], W[FQ]), dot_nn(shifts[2], W[FQ]), extra)
    crit_q = []
    for k in (2, 1, 3):
        t = others[k - 1]
        crit_q.append((t, rdma(qsc.at[t // 3], qbuf.at[g], YQC + k, YQC + g, group=t)))
    for t, copy in crit_q:
        @pl.when(t != 0)
        def _():
            copy.start()

    have(TO)
    crit_m = [rdma(mb.at[g], mb.at[g], YMC + k, YMC + g, group=others[k - 1]) for k in (1, 2, 3)]

    @pl.when(g != 0)
    def _():
        for o in others:
            y_wait(YQC, o, qbuf.at[o])
        total, bias, extra = gathered(qsc.at[g // 3])
        square = extra[:, 0:1] + extra[:, 64:65]
        r = lax.rsqrt(square * (1.0 / D) + EPSILON)
        ss_out[...] = jnp.broadcast_to(r, (TOK, 128))
        attend(r, total, bias)
        for copy in (crit_m[1], crit_m[0], crit_m[2]):
            copy.start()

    @pl.when(g == 0)
    def _():
        ss_out[...] = jnp.broadcast_to(r1[...], (TOK, 128))

    have(FO)
    for r in (1, 2, 3):
        @pl.when(g != r)
        def _():
            y_wait(YMC, r, mb.at[r])
        planes(r, TO if r < 3 else FO, mb.at[r])
        rs_first(r)
    for k in (2, 1, 3):
        y_send(YNO, k, G.at[0, slice_rows(m)], out4.at[2, g])
    gen_p = rdma(send_p.at[0], out4.at[0, g], YGN, YGN + g, group=0)

    @pl.when(g != 0)
    def _():
        gen_p.start()

    for r in (1, 2, 3):
        rs_second(r)
    own_n = G[0, slice_rows(m), :].astype(F32)
    for r in (1, 2, 3):
        gate = gate_t if r < 3 else gate_f
        send_p[r] = (own_n + gate * rs_total(r)).astype(BF)
    crit_p = []
    for k in (2, 1, 3):
        t = others[k - 1]
        crit_p.append((t, rdma(send_p.at[t], out4.at[0, g], YPR + k, YPR + g, group=t)))

    cond, uncond, faked = [send_p[r].astype(F32) for r in (1, 2, 3)]
    real = GUIDANCE * cond - (GUIDANCE - 1.0) * uncond
    score = faked - real
    score_b = score.astype(BF)
    gen_cot = dot_nt(score_b, onehot[...])
    send_c[0] = gen_cot.astype(BF)
    send_c[1] = score_b
    send_c[2] = score_b
    fake_cot = faked - arr
    send_c[3] = fake_cot.astype(BF)
    mine = slice_rows(m)
    G[1, mine, :] = (gate_g * gen_cot).astype(BF)
    ag_first(1)
    G[2, mine, :] = (gate_t * score).astype(BF)
    ag_first(2)
    G[3, mine, :] = (gate_f * fake_cot).astype(BF)
    ag_first(3)
    dist = jnp.sum(jnp.abs(arr - real), axis=0, keepdims=True)
    dist = dist[:, 0:128] + dist[:, 128:256]
    dsend[0] = jnp.broadcast_to(dist, (8, 128))
    for t, copy in crit_p:
        @pl.when(t != 0)
        def _():
            copy.start()

    def butterfly(step):
        where = [dict(mp=m_core), dict(mp=m_x), dict(seq=s_x), dict(seq=s_pair), dict(seq=s_far)][step]
        return rdma(dsend.at[step], drecv.at[step], BUT + step, BUT + step, **where)

    def butterfly_end(step):
        rdma(drecv.at[step], drecv.at[step], BUT + step, BUT + step, mp=m_core).wait_recv()
        dsend[step + 1] = dsend[step] + drecv[step]

    start(butterfly(0))
    for r in (1, 2, 3):
        ag_second(r)
    for r, k in ((1, GO), (2, TO), (3, FO)):
        ag_wait(r)
        gms[r - 1] = dot_tn(G[r], W[k]).astype(BF)
    for k in (2, 1, 3):
        t = others[k - 1]
        y_send(YGM, k, gms.at[(t + 1) // 2], gmb.at[g])
    butterfly_end(0)
    start(butterfly(1))

    for o in others:
        y_wait(YGM, o, gmb.at[o])
    total = gms[(g + 1) // 2].astype(F32)
    for o in others:
        total = total + gmb[o].astype(F32)
    factor = jnp.where(g == 1, -GUIDANCE, jnp.where(g == 2, GUIDANCE - 1.0, 1.0)).astype(F32)
    gmb[g] = (total * factor).astype(BF)

    def head_back(h, inner):
        lanes = lanes_of(h)
        qh = qq[:, lanes]
        rq = lax.rsqrt(jnp.mean(qh * qh, axis=1, keepdims=True) + EPSILON)
        unit = qh * rq
        w = probs[h].astype(F32)
        dp = dot_nt(gmb[g, :, lanes], values[:, lanes])
        gs = (w * (dp - jnp.sum(w * dp, axis=1, keepdims=True))).astype(BF)
        dqn = dot_nn(gs, keys[:, lanes]) * scaling
        grad = rq * (dqn - unit * jnp.mean(unit * dqn, axis=1, keepdims=True))
        gq[g, :, lanes] = grad.astype(BF)
        return inner + jnp.sum(grad * qA[:, lanes], axis=1, keepdims=True)

    inner = lax.fori_loop(0, HEADS, head_back, jnp.zeros((TOK, 1), F32))
    for k in (2, 1, 3):
        y_send(YGQ, k, gq.at[g], gq.at[g])
    isend[0] = jnp.broadcast_to(inner, (TOK, 128))
    start(rdma(isend.at[0], irecv.at[0], INN, INN, mp=m_core))
    butterfly_end(1)
    start(butterfly(2))
    rdma(irecv.at[0], irecv.at[0], INN, INN, mp=m_core).wait_recv()
    isend[1] = isend[0] + irecv[0]
    start(rdma(isend.at[1], irecv.at[1], INN + 1, INN + 1, mp=m_x))
    butterfly_end(2)
    start(butterfly(3))

    for r in range(4):
        @pl.when(g != r)
        def _():
            y_wait(YGQ, r, gq.at[r])
        planes(4 + r, (GQ, TQ, TQ, FQ)[r], gq.at[r])
        rs_first(4 + r)
    butterfly_end(3)
    start(butterfly(4))
    for r in range(4):
        rs_second(4 + r)
    for k in (2, 1, 3):
        t = others[k - 1]
        y_send(YCO, k, send_c.at[t], out4.at[1, g])
    for r in range(4):
        send_h[r] = rs_total(4 + r).astype(BF)
    for k in (2, 1, 3):
        t = others[k - 1]
        y_send(YGH, k, send_h.at[t], out4.at[3, g])
    butterfly_end(4)
    for k in (2, 1, 3):
        y_send(YDI, k, dsend.at[5], drecv.at[5 + g])
    rdma(irecv.at[1], irecv.at[1], INN + 1, INN + 1, mp=m_x).wait_recv()
    inner_out[...] = isend[1] + irecv[1]
    out4[0, g] = send_p[g]
    out4[1, g] = send_c[g]
    out4[2, g] = G[0, mine, :]
    out4[3, g] = send_h[g]
    total = dsend[5]
    for o in others:
        y_wait(YDI, o, drecv.at[5 + o])
        total = total + drecv[5 + o]
    dist_out[...] = total

    for o in others:
        y_wait(YNO, o, out4.at[2, o])
        y_wait(YCO, o, out4.at[1, o])
        y_wait(YGH, o, out4.at[3, o])

    @pl.when(g == 0)
    def _():
        for o in others:
            y_wait(YGN, o, out4.at[0, o])
        for copy in gen_m:
            copy.wait_send()

    @pl.when(g != 0)
    def _():
        for o in others:
            y_wait(YPR, o, out4.at[0, o])
        gen_q.wait_send()
        gen_p.wait_send()
        for copy in crit_m:
            copy.wait_send()

    for t, copy in crit_q + crit_p:
        @pl.when(t != 0)
        def _():
            copy.wait_send()

    for copy in pending:
        copy.wait_send()


def fused(*operands):
    vmem = pl.BlockSpec(memory_space=pltpu.VMEM)
    act = lambda *lead: pltpu.VMEM(lead + (SLICE, TOK), BF)
    return pl.pallas_call(
        kernel,
        out_shape=[
            jax.ShapeDtypeStruct((4, 4, SLICE, TOK), BF),
            jax.ShapeDtypeStruct((TOK, 128), F32),
            jax.ShapeDtypeStruct((TOK, 128), F32),
            jax.ShapeDtypeStruct((8, 128), F32),
        ],
        in_specs=[vmem] * len(operands),
        out_specs=[vmem] * 4,
        scratch_shapes=[
            pltpu.VMEM((6, QUARTER, COLS), BF),
            pltpu.VMEM((QROWS, QCOLS), BF),
            pltpu.VMEM((2, QROWS, QCOLS), BF),
            pltpu.VMEM((4, QROWS, QCOLS), BF),
            pltpu.VMEM((TOK, COLS), F32),
            pltpu.VMEM((TOK, COLS), F32),
            pltpu.VMEM((HEADS, TOK, TEXT), BF),
            pltpu.VMEM((4, TOK, COLS), BF),
            pltpu.VMEM((8, QUARTER, TOK), BF),
            act(8, 2),
            act(8),
            act(8),
            pltpu.VMEM((4, QUARTER, TOK), BF),
            pltpu.VMEM((2, QUARTER, TOK), BF),
            act(4),
            act(4),
            act(4),
            pltpu.VMEM((3, TOK, COLS), BF),
            pltpu.VMEM((4, TOK, COLS), BF),
            pltpu.VMEM((4, TOK, COLS), BF),
            pltpu.VMEM((2, TOK, 128), F32),
            pltpu.VMEM((2, TOK, 128), F32),
            pltpu.VMEM((6, 8, 128), F32),
            pltpu.VMEM((9, 8, 128), F32),
            pltpu.SemaphoreType.DMA((N_SEM,)),
            pltpu.SemaphoreType.DMA((N_SEM,)),
        ],
        compiler_params=pltpu.CompilerParams(
            collective_id=0, has_side_effects=True, vmem_limit_bytes=60 * 2**20
        ),
        cost_estimate=pl.CostEstimate(flops=8 * 10**9, bytes_accessed=10**7, transcendentals=10**6),
    )(*operands)


def on_device(
    gen_input, noise, gen_steps, critic_steps, row_order,
    gen_wq, gen_wo, teacher_wq, teacher_wo, fake_wq, fake_wo,
    gen_mod, teacher_mod, fake_mod, text_keys, text_values,
):
    g = lax.axis_index("group")
    s = lax.axis_index("seq")
    m = lax.axis_index("mp")
    sample = s // (lax.axis_size("seq") // SAMPLES)
    is_gen = g == 0
    is_fake = g == GROUPS - 1
    step_count = gen_mod.shape[0]

    def pick(values, index, axis):
        return lax.dynamic_index_in_dim(values, index, axis, keepdims=False)

    def quarter(values):
        return pick(values.reshape(values.shape[:-1] + (16, 4, SUB)), g, values.ndim).reshape(
            values.shape[:-1] + (QUARTER,)
        )

    def own_slice(values):
        return lax.dynamic_slice_in_dim(values, m * SLICE, SLICE, values.ndim - 1)

    def block(values):
        return lax.dynamic_slice_in_dim(values, m * QUARTER, QUARTER, values.ndim - 1)

    gen_step = pick(gen_steps, sample, 0)
    critic_step = pick(critic_steps, sample, 0)
    mod_g = pick(gen_mod, gen_step, 0).astype(F32)
    mod_t = pick(teacher_mod, critic_step, 0).astype(F32)
    mod_f = pick(fake_mod, critic_step, 0).astype(F32)
    quarter_g, quarter_t, quarter_f = quarter(mod_g), quarter(mod_t), quarter(mod_f)

    x = gen_input.astype(F32)
    r1 = lax.rsqrt(jnp.mean(x * x, axis=1, keepdims=True) + EPSILON)
    xq = quarter(gen_input)
    a1 = (xq.astype(F32) * (1.0 + quarter_g[1])).astype(BF).T
    x1s = own_slice(xq).T
    nzs = own_slice(quarter(noise)).T
    order = row_order[0]
    onehot = (jnp.arange(TOK, dtype=jnp.int32)[:, None] == order[None, :]).astype(BF)
    shifts = jnp.broadcast_to(
        jnp.stack([quarter_g[0], quarter_t[0], quarter_f[0]])[:, None, :], (3, 16, QUARTER)
    ).astype(BF)
    angle = 0.5 * jnp.pi * (critic_step.astype(F32) + 1.0) / (step_count + 1.0)
    cols = jnp.stack([1.0 + quarter_t[1], 1.0 + quarter_f[1]], axis=1)
    ones = jnp.ones((SLICE,), F32)
    scols = jnp.stack(
        [own_slice(quarter_g[2]), own_slice(quarter_t[2]), own_slice(quarter_f[2]),
         ones * jnp.cos(angle), ones * jnp.sin(angle)], axis=1)
    wown = jnp.stack([
        lax.dynamic_slice_in_dim(w, g * SUB, SUB, 0)
        for w in (gen_wq, gen_wo, teacher_wq, fake_wq, teacher_wo, fake_wo)
    ])
    kf = text_keys[0].astype(F32).reshape(TEXT, HEADS, HEAD)
    keys = (kf * lax.rsqrt(jnp.mean(kf * kf, axis=2, keepdims=True) + EPSILON)).astype(BF)
    keys = keys.reshape(TEXT, COLS)

    out4, r_cols, inner_cols, dist = fused(
        wown, a1, x1s, nzs, onehot, shifts, cols, scols, r1, keys, text_values[0]
    )
    rows = out4.reshape(4, 4, 4, SUB, TOK).transpose(0, 4, 2, 1, 3).reshape(4, TOK, QUARTER)
    predictions = rows[0]
    cot, noised, grad_hidden = rows[1].astype(F32), rows[2].astype(F32), rows[3].astype(F32)
    r = r_cols[:, 0:1]
    inner = inner_cols[:, 0:1] * (1.0 / D)
    sample_size = float(TOK * lax.axis_size("seq") // SAMPLES * D)
    denominator = jnp.sum(dist[0]) / sample_size + FLOOR_EPSILON
    scale = block(jnp.where(is_gen, mod_g[1], jnp.where(is_fake, mod_f[1], mod_t[1])))
    x_rows = jnp.where(is_gen, block(x), noised)
    factor = jnp.where(g == 1, -GUIDANCE, jnp.where(g == 2, GUIDANCE - 1.0, 1.0))
    grads = factor * cot + r * (1.0 + scale) * grad_hidden - x_rows * (r * r * r * inner)
    grads = grads * jnp.where(is_fake, 1.0, 1.0 / denominator)
    return (predictions[None], grads[None])


def solution(mesh):
    placed = (
        P("seq", None),
        P("seq", None),
        P(),
        P(),
        P("seq", None),
        P("seq", "mp"),
        P("seq", "mp"),
        P("seq", "mp"),
        P("seq", "mp"),
        P("seq", "mp"),
        P("seq", "mp"),
        P(),
        P(),
        P(),
        P("group", None, "mp"),
        P("group", None, "mp"),
    )
    return jax.shard_map(
        on_device,
        mesh=mesh,
        in_specs=placed,
        out_specs=(P("group", "seq", "mp"), P("group", "seq", "mp")),
        check_vma=False,
    )
```

```python
import jax
import jax.numpy as jnp
from jax import lax
from jax.experimental import pallas as pl
from jax.experimental.pallas import tpu as pltpu
from jax.sharding import PartitionSpec as P

D = 5120
HEAD = 128
SAMPLES = 2
GROUPS = 4
TOK = 256
TEXT = 512
COLS = 640
HEADS = 5
SUB = 80
SLICE = 320
QUARTER = 1280
QROWS = TOK + 16
LAG = 3
EPSILON = 1e-06
FLOOR_EPSILON = 1e-05
GUIDANCE = 3.0
BF = jnp.bfloat16
F32 = jnp.float32

GQ, GO, TQ, FQ, TO, FO = range(6)


def dot_nn(a, b):
    return lax.dot_general(a, b, (((1,), (0,)), ((), ())), preferred_element_type=F32)


def dot_nt(a, b):
    return lax.dot_general(a, b, (((1,), (1,)), ((), ())), preferred_element_type=F32)


def dot_tn(a, b):
    return lax.dot_general(a, b, (((0,), (0,)), ((), ())), preferred_element_type=F32)


class Slots:
    def __init__(self):
        self.count = 0

    def take(self, number):
        first = self.count
        self.count += number
        return first


SLOTS = Slots()
RING = SLOTS.take(2 * 6 * 7)
XCH = SLOTS.take(6)
YQG = SLOTS.take(4)
YQC = SLOTS.take(4)
YMG = SLOTS.take(4)
YMC = SLOTS.take(4)
YPR = SLOTS.take(4)
YGN = SLOTS.take(4)
YRR = SLOTS.take(4)
YIN = SLOTS.take(4)
YGM = SLOTS.take(4)
YGQ = SLOTS.take(4)
YGH = SLOTS.take(4)
YDI = SLOTS.take(4)
RSC = SLOTS.take(8 * 2)
RSX = SLOTS.take(8)
AGM = SLOTS.take(4 * 3)
BUT = SLOTS.take(5)
INN = SLOTS.take(2)
N_SEM = SLOTS.count


def kernel(
    gen_steps, critic_steps, row_order, gen_input, noise,
    w_gq, w_go, w_tq, w_to, w_fq, w_fo, tab_g, tab_t, tab_f, text_keys, text_values,
    out_p, out_g,
    W, qsg, qsc, qbuf, qA, qq, probs, mb, PP, CC, SS, XX, G, an,
    xv, nv, tg, tt, tf, kraw, keys, values, modv, sel, xT, onehot, colsT,
    send_p, send_f, pbuf, fbuf, cots, gms, gmb, gq, rsend, rrecv, isend, irecv, irow, dsend, drecv,
    ssem, rsem, lsem,
):
    g = lax.axis_index("group")
    s = lax.axis_index("seq")
    m = lax.axis_index("mp")
    z, xh = s // 2, lax.rem(s, 2)
    xl, c = m // 2, lax.rem(m, 2)
    m_core = 2 * xl + 1 - c
    m_x = 2 * (1 - xl) + c
    s_x = 2 * z + 1 - xh
    z_pair = z + 1 - 2 * lax.rem(z, 2)
    z_far = z + 2 - 4 * lax.rem(z // 2, 2)
    s_up = lax.rem(z + 1, 8) * 2 + xh
    s_down = lax.rem(z + 7, 8) * 2 + xh
    s_pair = z_pair * 2 + xh
    s_far = z_far * 2 + xh
    others = [lax.rem(g + k, GROUPS) for k in (1, 2, 3)]
    pending = []
    own_w = [w.at[pl.ds(pl.multiple_of(g * SUB, 16), SUB)] for w in (w_gq, w_go, w_tq, w_fq, w_to, w_fo)]
    sample = s // 8

    def rdma(src, dst, send, recv, **where):
        return pltpu.make_async_remote_copy(
            src_ref=src, dst_ref=dst, send_sem=ssem.at[send], recv_sem=rsem.at[recv],
            device_id=where, device_id_type=pl.DeviceIdType.MESH,
        )

    def start(copy):
        copy.start()
        pending.append(copy)

    mine_of_d = pl.ds(pl.multiple_of(m * QUARTER, 128), QUARTER)
    loads = [
        pltpu.make_async_copy(gen_input, xv, lsem.at[0]),
        pltpu.make_async_copy(tab_g, tg, lsem.at[1]),
        pltpu.make_async_copy(tab_t, tt, lsem.at[2]),
        pltpu.make_async_copy(tab_f, tf, lsem.at[3]),
        pltpu.make_async_copy(text_keys.at[0], kraw, lsem.at[4]),
        pltpu.make_async_copy(text_values.at[0], values, lsem.at[5]),
        pltpu.make_async_copy(noise.at[:, mine_of_d], nv, lsem.at[6]),
    ]

    barrier = pltpu.get_barrier_semaphore()
    peers = [{"group": o} for o in others]
    peers += [{"mp": m_core}, {"mp": m_x}, {"seq": s_x}, {"seq": s_up}, {"seq": s_down}, {"seq": s_far}]
    for peer in peers:
        pl.semaphore_signal(barrier, inc=1, device_id=peer, device_id_type=pl.DeviceIdType.MESH)
    pl.semaphore_wait(barrier, len(peers))

    def rows_of(zz, x):
        return pl.ds(pl.multiple_of((lax.rem(zz + 16, 8) * 2 + x) * SUB, 16), SUB)

    def ring_copy(way, k, t):
        sem = RING + (way * 6 + k) * 7 + t
        if way == 0:
            rows = rows_of(z - t, xh)
            src = own_w[k] if t == 0 else W.at[k, rows]
            return rdma(src, W.at[k, rows], sem, sem, seq=s_up)
        rows = rows_of(z + t, 1 - xh)
        return rdma(W.at[k, rows], W.at[k, rows], sem, sem, seq=s_down)

    def ring_wait(way, k, t):
        sem = RING + (way * 6 + k) * 7 + t
        rows = rows_of(z - 1 - t, xh) if way == 0 else rows_of(z + 1 + t, 1 - xh)
        rdma(W.at[k, rows], W.at[k, rows], sem, sem, seq=s_up).wait_recv()

    my_rows = rows_of(z, xh)
    for k in range(6):
        start(rdma(own_w[k], W.at[k, my_rows], XCH + k, XCH + k, seq=s_x))
    own_loads = [pltpu.make_async_copy(own_w[k], W.at[k, my_rows], lsem.at[7 + k]) for k in range(6)]

    state = {"tick": 0}

    def ring_to(last):
        while state["tick"] <= last:
            tick = state["tick"]
            for k in range(6):
                t = tick - LAG * k
                if t == 0:
                    start(ring_copy(0, k, 0))
                    other = rows_of(z, 1 - xh)
                    rdma(W.at[k, other], W.at[k, other], XCH + k, XCH + k, seq=s_x).wait_recv()
                    start(ring_copy(1, k, 0))
            for k in range(6):
                t = tick - LAG * k
                if 0 <= t <= 6:
                    for way in (0, 1):
                        ring_wait(way, k, t)
                        if t < 6:
                            start(ring_copy(way, k, t + 1))
            state["tick"] += 1

    def have(k):
        ring_to(LAG * k + 6)
        own_loads[k].wait()

    def y_send(base, dg, src, dst):
        start(rdma(src, dst, base + dg, base + g, group=others[dg - 1]))

    def y_wait(base, source, ref):
        rdma(ref, ref, base, base + source, group=others[0]).wait_recv()

    def slice_rows(index):
        return pl.ds(pl.multiple_of(index * SLICE, 16), SLICE)

    def rs_first(r):
        for far in (1, 0):
            x = 1 - xl if far else xl
            start(rdma(PP.at[r, slice_rows(2 * x + 1 - c)], CC.at[r, x],
                       RSC + 2 * r + far, RSC + 2 * r + x, mp=m_core))

    def rs_core_wait(r, x):
        rdma(CC.at[r, x], CC.at[r, x], RSC + 2 * r, RSC + 2 * r + x, mp=m_core).wait_recv()

    def rs_second(r):
        rs_core_wait(r, 1 - xl)
        SS[r] = (PP[r, slice_rows(2 * (1 - xl) + c), :].astype(F32) + CC[r, 1 - xl].astype(F32)).astype(BF)
        start(rdma(SS.at[r], XX.at[r], RSX + r, RSX + r, mp=m_x))

    def rs_total(r):
        rs_core_wait(r, xl)
        rdma(XX.at[r], XX.at[r], RSX + r, RSX + r, mp=m_x).wait_recv()
        return (PP[r, slice_rows(m), :].astype(F32) + CC[r, xl].astype(F32)) + XX[r].astype(F32)

    def ag_first(r):
        rows = slice_rows(m)
        start(rdma(G.at[r, rows], G.at[r, rows], AGM + 3 * r, AGM + 3 * r, mp=m_x))
        start(rdma(G.at[r, rows], G.at[r, rows], AGM + 3 * r + 1, AGM + 3 * r + 1, mp=m_core))

    def ag_second(r):
        rows = slice_rows(m_x)
        rdma(G.at[r, rows], G.at[r, rows], AGM + 3 * r, AGM + 3 * r, mp=m_x).wait_recv()
        start(rdma(G.at[r, rows], G.at[r, rows], AGM + 3 * r + 2, AGM + 3 * r + 2, mp=m_core))

    def ag_wait(r):
        for extra, index in ((1, m_core), (2, 2 * (1 - xl) + 1 - c)):
            rows = slice_rows(index)
            rdma(G.at[r, rows], G.at[r, rows], AGM + 3 * r + extra, AGM + 3 * r + extra, mp=m_core).wait_recv()

    def planes(r, k, ref):
        def body(i, carry):
            rows = slice_rows(i)
            PP[r, rows, :] = dot_nt(W[k, rows, :], ref[...]).astype(BF)
            return carry
        lax.fori_loop(0, 4, body, 0)

    scaling = HEAD ** -0.5

    def lanes_of(h):
        return pl.ds(pl.multiple_of(h * HEAD, HEAD), HEAD)

    def attend(r, total, bias):
        qA[...] = total
        qq[...] = r * total + bias

        def head(h, carry):
            lanes = lanes_of(h)
            qh = qq[:, lanes]
            rq = lax.rsqrt(jnp.mean(qh * qh, axis=1, keepdims=True) + EPSILON)
            e = jnp.exp(dot_nt((qh * rq).astype(BF), keys[:, lanes]) * scaling)
            p = (e * (1.0 / jnp.sum(e, axis=1, keepdims=True))).astype(BF)
            probs[h] = p
            mb[g, :, lanes] = dot_nn(p, values[:, lanes]).astype(BF)
            return carry

        lax.fori_loop(0, HEADS, head, 0)

    def gathered(own):
        parts = [own] + [qbuf.at[o] for o in others]
        total = sum(p[0:TOK, :].astype(F32) for p in parts)
        bias = sum(p[TOK:QROWS, :].astype(F32) for p in parts)[0:1, :]
        return total, bias

    def to_bf_rows(ref, part, bias):
        ref[0:TOK, :] = part.astype(BF)
        ref[TOK:QROWS, :] = jnp.broadcast_to(bias, (16, COLS)).astype(BF)

    ring_to(0)
    for copy in loads + own_loads:
        copy.start()
    row = lax.broadcasted_iota(jnp.int32, (2 * SUB, 2 * SLICE), 0)
    col = lax.broadcasted_iota(jnp.int32, (2 * SUB, 2 * SLICE), 1)
    base = row + jnp.where(row >= SUB, SLICE - SUB, 0)
    for o in range(4):
        sel[o] = (col == base + o * SUB).astype(BF)
    order = lax.broadcasted_iota(jnp.int32, (TOK, TOK), 0)
    onehot[...] = (order == row_order[...]).astype(BF)
    modv[...] = jnp.zeros_like(modv)
    for copy in loads:
        copy.wait()
    modv[0:3, :] = tg[gen_steps[sample]].astype(F32)
    modv[3:6, :] = tt[critic_steps[sample]].astype(F32)
    modv[6:9, :] = tf[critic_steps[sample]].astype(F32)
    own_sel = sel[g]
    square_row = jnp.zeros((8, TOK), F32)
    square_col = jnp.zeros((TOK, 128), F32)
    for w in range(8):
        window = pl.ds(w * 2 * SLICE, 2 * SLICE)
        rows = pl.ds(w * 2 * SUB, 2 * SUB)
        part = xv[:, window]
        xw = dot_nt(own_sel, part)
        cw = dot_nt(own_sel, modv[:, window].astype(BF))
        colsT[rows, :] = cw
        xT[rows, :] = xw.astype(BF)
        an[0, rows, :] = (xw * (1.0 + cw[:, 1:2])).astype(BF)
        sq = part.astype(F32)
        sq = (sq * sq).astype(BF)
        square_row = square_row + dot_nt(jnp.ones((8, 2 * SLICE), BF), sq)
        square_col = square_col + dot_nn(sq, jnp.ones((2 * SLICE, 128), BF))
    r1_row = lax.rsqrt(square_row[0:1, :] * (1.0 / D) + EPSILON)
    r1 = lax.rsqrt(square_col[:, 0:1] * (1.0 / D) + EPSILON)
    for h in range(HEADS):
        lanes = pl.ds(h * HEAD, HEAD)
        kf = kraw[:, lanes].astype(F32)
        keys[:, lanes] = (kf * lax.rsqrt(jnp.mean(kf * kf, axis=1, keepdims=True) + EPSILON)).astype(BF)
    cols_b = colsT[...].astype(BF)
    mine = slice_rows(m)
    scols = colsT[mine, :]
    gate_g, gate_t, gate_f = scols[:, 2:3], scols[:, 5:6], scols[:, 8:9]
    angle = jnp.full((8, 128), critic_steps[sample] + 1).astype(F32) * (0.5 * 3.141592653589793 / (tg.shape[0] + 1.0))
    alpha, sigma = jnp.cos(angle)[0:1, 0:1], jnp.sin(angle)[0:1, 0:1]
    have(GQ)
    to_bf_rows(qsg, dot_tn(an[0], W[GQ]), dot_tn(cols_b, W[GQ])[0:1])
    gen_q = rdma(qsg, qbuf.at[g], YQG, YQG + g, group=0)

    @pl.when(g != 0)
    def _():
        gen_q.start()

    have(GO)

    gen_m = [rdma(mb.at[0], mb.at[0], YMG + k, YMG, group=others[k - 1]) for k in (1, 2, 3)]

    @pl.when(g == 0)
    def _():
        for o in others:
            y_wait(YQG, o, qbuf.at[o])
        total, bias = gathered(qsg)
        attend(r1, total, bias)
        for copy in (gen_m[1], gen_m[0], gen_m[2]):
            copy.start()

    ring_to(LAG * TQ + 6)

    @pl.when(g != 0)
    def _():
        y_wait(YMG, 0, mb.at[0])

    planes(0, GO, mb.at[0])
    rs_first(0)
    rs_second(0)
    total = rs_total(0)
    gen_s = (xT[mine, :].astype(F32) + gate_g * total).astype(BF)
    send_p[0] = gen_s
    arr = dot_nn(gen_s, onehot[...])
    nzs = jnp.concatenate([dot_nt(own_sel, nv[:, pl.ds(w * 2 * SLICE, 2 * SLICE)]) for w in (0, 1)], axis=0)
    noised = (alpha * arr + sigma * nzs).astype(BF)
    G[0, mine, :] = noised
    ag_first(0)
    ag_second(0)
    ag_wait(0)

    nf = G[0].astype(F32)
    sq = (nf * nf).astype(BF)
    rsend[...] = dot_nn(jnp.ones((8, QUARTER), BF), sq)
    for k in (2, 1, 3):
        y_send(YRR, k, rsend, rrecv.at[g])
    an[0] = (nf * (1.0 + colsT[:, 4:5])).astype(BF)
    an[1] = (nf * (1.0 + colsT[:, 7:8])).astype(BF)
    have(TQ)
    to_bf_rows(qsc.at[0], dot_tn(an[0], W[TQ]), dot_tn(cols_b, W[TQ])[3:4])
    have(FQ)
    to_bf_rows(qsc.at[1], dot_tn(an[1], W[FQ]), dot_tn(cols_b, W[FQ])[6:7])
    crit_q = []
    for k in (2, 1, 3):
        t = others[k - 1]
        crit_q.append((t, rdma(qsc.at[t // 3], qbuf.at[g], YQC + k, YQC + g, group=t)))
    for t, copy in crit_q:
        @pl.when(t != 0)
        def _():
            copy.start()

    have(TO)
    square_row = rsend[...]
    for o in others:
        y_wait(YRR, o, rrecv.at[o])
        square_row = square_row + rrecv[o]
    rn_row = lax.rsqrt(square_row[0:1, :] * (1.0 / D) + EPSILON)
    crit_m = [rdma(mb.at[g], mb.at[g], YMC + k, YMC + g, group=others[k - 1]) for k in (1, 2, 3)]

    @pl.when(g != 0)
    def _():
        for o in others:
            y_wait(YQC, o, qbuf.at[o])
        total, bias = gathered(qsc.at[g // 3])
        attend(jnp.transpose(jnp.broadcast_to(rn_row, (128, TOK)))[:, 0:1], total, bias)
        for copy in (crit_m[1], crit_m[0], crit_m[2]):
            copy.start()

    have(FO)
    for r in (1, 2, 3):
        @pl.when(g != r)
        def _():
            y_wait(YMC, r, mb.at[r])
        planes(r, TO if r < 3 else FO, mb.at[r])
        rs_first(r)
    gen_p = rdma(send_p.at[0], pbuf.at[g], YGN, YGN + g, group=0)

    @pl.when(g != 0)
    def _():
        gen_p.start()

    for r in (1, 2, 3):
        rs_second(r)
    own_n = G[0, slice_rows(m), :].astype(F32)
    for r in (1, 2, 3):
        gate = gate_t if r < 3 else gate_f
        send_p[r] = (own_n + gate * rs_total(r)).astype(BF)
    crit_p = []
    for k in (2, 1, 3):
        t = others[k - 1]
        crit_p.append((t, rdma(send_p.at[t], pbuf.at[g], YPR + k, YPR + g, group=t)))

    cond, uncond, faked = [send_p[r].astype(F32) for r in (1, 2, 3)]
    real = GUIDANCE * cond - (GUIDANCE - 1.0) * uncond
    score = faked - real
    score_b = score.astype(BF)
    gen_cot = dot_nt(score_b, onehot[...])
    fake_cot = faked - arr
    cots[0] = gen_cot
    cots[1] = score
    cots[2] = fake_cot
    G[1, mine, :] = (gate_g * gen_cot).astype(BF)
    ag_first(1)
    G[2, mine, :] = (gate_t * score).astype(BF)
    ag_first(2)
    G[3, mine, :] = (gate_f * fake_cot).astype(BF)
    ag_first(3)
    dist = jnp.sum(jnp.abs(arr - real), axis=0, keepdims=True)
    dist = dist[:, 0:128] + dist[:, 128:256]
    dsend[0] = jnp.broadcast_to(dist, (8, 128))
    for t, copy in crit_p:
        @pl.when(t != 0)
        def _():
            copy.start()

    def butterfly(step):
        where = [dict(mp=m_core), dict(mp=m_x), dict(seq=s_x), dict(seq=s_pair), dict(seq=s_far)][step]
        return rdma(dsend.at[step], drecv.at[step], BUT + step, BUT + step, **where)

    def butterfly_end(step):
        rdma(drecv.at[step], drecv.at[step], BUT + step, BUT + step, mp=m_core).wait_recv()
        dsend[step + 1] = dsend[step] + drecv[step]

    start(butterfly(0))
    for r in (1, 2, 3):
        ag_second(r)
    for r, k in ((1, GO), (2, TO), (3, FO)):
        ag_wait(r)
        gms[r - 1] = dot_tn(G[r], W[k]).astype(BF)
    for k in (2, 1, 3):
        t = others[k - 1]
        y_send(YGM, k, gms.at[(t + 1) // 2], gmb.at[g])
    butterfly_end(0)
    start(butterfly(1))

    for o in others:
        y_wait(YGM, o, gmb.at[o])
    total = gms[(g + 1) // 2].astype(F32)
    for o in others:
        total = total + gmb[o].astype(F32)
    factor = jnp.where(g == 1, -GUIDANCE, jnp.where(g == 2, GUIDANCE - 1.0, 1.0)).astype(F32)
    gmb[g] = (total * factor).astype(BF)

    def head_back(h, inner):
        lanes = lanes_of(h)
        qh = qq[:, lanes]
        rq = lax.rsqrt(jnp.mean(qh * qh, axis=1, keepdims=True) + EPSILON)
        unit = qh * rq
        w = probs[h].astype(F32)
        dp = dot_nt(gmb[g, :, lanes], values[:, lanes])
        gs = (w * (dp - jnp.sum(w * dp, axis=1, keepdims=True))).astype(BF)
        dqn = dot_nn(gs, keys[:, lanes]) * scaling
        grad = rq * (dqn - unit * jnp.mean(unit * dqn, axis=1, keepdims=True))
        gq[g, :, lanes] = grad.astype(BF)
        return inner + jnp.sum(grad * qA[:, lanes], axis=1, keepdims=True)

    inner = lax.fori_loop(0, HEADS, head_back, jnp.zeros((TOK, 1), F32))
    for k in (2, 1, 3):
        y_send(YGQ, k, gq.at[g], gq.at[g])
    isend[0] = jnp.transpose(jnp.broadcast_to(inner, (TOK, 128)))[0:8, :]
    start(rdma(isend.at[0], irecv.at[0], INN, INN, mp=m_core))
    butterfly_end(1)
    start(butterfly(2))
    rdma(irecv.at[0], irecv.at[0], INN, INN, mp=m_core).wait_recv()
    isend[1] = isend[0] + irecv[0]
    start(rdma(isend.at[1], irecv.at[1], INN + 1, INN + 1, mp=m_x))
    butterfly_end(2)
    start(butterfly(3))
    rdma(irecv.at[1], irecv.at[1], INN + 1, INN + 1, mp=m_x).wait_recv()
    irow[g] = isend[1] + irecv[1]
    for k in (2, 1, 3):
        y_send(YIN, k, irow.at[g], irow.at[g])

    for r in range(4):
        @pl.when(g != r)
        def _():
            y_wait(YGQ, r, gq.at[r])
        planes(4 + r, (GQ, TQ, TQ, FQ)[r], gq.at[r])
        rs_first(4 + r)
    butterfly_end(3)
    start(butterfly(4))
    for r in range(4):
        rs_second(4 + r)
    butterfly_end(4)
    for k in (2, 1, 3):
        y_send(YDI, k, dsend.at[5], drecv.at[5 + g])
    total = dsend[5]
    for o in others:
        y_wait(YDI, o, drecv.at[5 + o])
        total = total + drecv[5 + o]
    count = float(TOK * 16 // SAMPLES * D)
    inverse = 1.0 / (jnp.sum(total[0:1, :], axis=1, keepdims=True) * (1.0 / count) + FLOOR_EPSILON)
    for o in others:
        y_wait(YIN, o, irow.at[o])
    for r in range(4):
        scale = 1.0 + scols[:, (1, 4, 4, 7)[r]:(1, 4, 4, 7)[r] + 1]
        rr = r1_row if r == 0 else rn_row
        rows = xT[mine, :].astype(F32) if r == 0 else own_n
        ct = (1.0, -GUIDANCE, GUIDANCE - 1.0, 1.0)[r] * cots[(0, 1, 1, 2)[r]]
        grads = ct + rr * scale * rs_total(4 + r) - rows * (rr * rr * rr * (irow[r][0:1, :] * (1.0 / D)))
        send_f[r] = (grads if r == 3 else grads * inverse).astype(BF)
    for k in (2, 1, 3):
        y_send(YGH, k, send_f.at[others[k - 1]], fbuf.at[g])
    pbuf[g] = send_p[g]
    fbuf[g] = send_f[g]

    def assemble(buf, w):
        rows = pl.ds(w * 2 * SUB, 2 * SUB)
        return sum(dot_tn(buf[o, rows, :], sel[o]) for o in range(4))

    @pl.when(g == 0)
    def _():
        for o in others:
            y_wait(YGN, o, pbuf.at[o])
        for copy in gen_m:
            copy.wait_send()

    @pl.when(g != 0)
    def _():
        for o in others:
            y_wait(YPR, o, pbuf.at[o])
        gen_q.wait_send()
        gen_p.wait_send()
        for copy in crit_m:
            copy.wait_send()

    for w in (0, 1):
        out_p[0, :, pl.ds(w * 2 * SLICE, 2 * SLICE)] = assemble(pbuf, w).astype(BF)
    for o in others:
        y_wait(YGH, o, fbuf.at[o])
    for w in (0, 1):
        out_g[0, :, pl.ds(w * 2 * SLICE, 2 * SLICE)] = assemble(fbuf, w)

    for t, copy in crit_q + crit_p:
        @pl.when(t != 0)
        def _():
            copy.wait_send()

    for copy in pending:
        copy.wait_send()


def on_device(*operands):
    vmem = pl.BlockSpec(memory_space=pltpu.VMEM)
    smem = pl.BlockSpec(memory_space=pltpu.SMEM)
    hbm = pl.BlockSpec(memory_space=pl.ANY)
    act = lambda *lead: pltpu.VMEM(lead + (SLICE, TOK), BF)
    (gen_input, noise, gen_steps, critic_steps, row_order) = operands[:5]
    table = pltpu.VMEM(operands[11].shape, BF)
    return pl.pallas_call(
        kernel,
        out_shape=[
            jax.ShapeDtypeStruct((1, TOK, QUARTER), BF),
            jax.ShapeDtypeStruct((1, TOK, QUARTER), F32),
        ],
        in_specs=[smem, smem, vmem] + [hbm] * 13,
        out_specs=[vmem] * 2,
        scratch_shapes=[
            pltpu.VMEM((6, QUARTER, COLS), BF),
            pltpu.VMEM((QROWS, COLS), BF),
            pltpu.VMEM((2, QROWS, COLS), BF),
            pltpu.VMEM((4, QROWS, COLS), BF),
            pltpu.VMEM((TOK, COLS), F32),
            pltpu.VMEM((TOK, COLS), F32),
            pltpu.VMEM((HEADS, TOK, TEXT), BF),
            pltpu.VMEM((4, TOK, COLS), BF),
            pltpu.VMEM((8, QUARTER, TOK), BF),
            act(8, 2),
            act(8),
            act(8),
            pltpu.VMEM((4, QUARTER, TOK), BF),
            pltpu.VMEM((2, QUARTER, TOK), BF),
            pltpu.VMEM((TOK, D), BF),
            pltpu.VMEM((TOK, QUARTER), BF),
            table,
            table,
            table,
            pltpu.VMEM((TEXT, COLS), BF),
            pltpu.VMEM((TEXT, COLS), BF),
            pltpu.VMEM((TEXT, COLS), BF),
            pltpu.VMEM((16, D), F32),
            pltpu.VMEM((4, 2 * SUB, 2 * SLICE), BF),
            pltpu.VMEM((QUARTER, TOK), BF),
            pltpu.VMEM((TOK, TOK), BF),
            pltpu.VMEM((QUARTER, 16), F32),
            act(4),
            act(4),
            act(4),
            act(4),
            pltpu.VMEM((3, SLICE, TOK), F32),
            pltpu.VMEM((3, TOK, COLS), BF),
            pltpu.VMEM((4, TOK, COLS), BF),
            pltpu.VMEM((4, TOK, COLS), BF),
            pltpu.VMEM((8, TOK), F32),
            pltpu.VMEM((4, 8, TOK), F32),
            pltpu.VMEM((2, 8, TOK), F32),
            pltpu.VMEM((2, 8, TOK), F32),
            pltpu.VMEM((4, 8, TOK), F32),
            pltpu.VMEM((6, 8, 128), F32),
            pltpu.VMEM((9, 8, 128), F32),
            pltpu.SemaphoreType.DMA((N_SEM,)),
            pltpu.SemaphoreType.DMA((N_SEM,)),
            pltpu.SemaphoreType.DMA((13,)),
        ],
        compiler_params=pltpu.CompilerParams(
            collective_id=0, has_side_effects=True, vmem_limit_bytes=60 * 2**20
        ),
        cost_estimate=pl.CostEstimate(flops=8 * 10**9, bytes_accessed=10**7, transcendentals=10**6),
    )(gen_steps, critic_steps, row_order, gen_input, noise, *operands[5:])


def solution(mesh):
    placed = (
        P("seq", None),
        P("seq", None),
        P(),
        P(),
        P("seq", None),
        P("seq", "mp"),
        P("seq", "mp"),
        P("seq", "mp"),
        P("seq", "mp"),
        P("seq", "mp"),
        P("seq", "mp"),
        P(),
        P(),
        P(),
        P("group", None, "mp"),
        P("group", None, "mp"),
    )
    return jax.shard_map(
        on_device,
        mesh=mesh,
        in_specs=placed,
        out_specs=(P("group", "seq", "mp"), P("group", "seq", "mp")),
        check_vma=False,
    )
```

```python
import jax
import jax.numpy as jnp
from jax import lax
from jax.experimental import pallas as pl
from jax.experimental.pallas import tpu as pltpu
from jax.sharding import PartitionSpec as P

D = 5120
HEAD = 128
SAMPLES = 2
GROUPS = 4
TOK = 256
TEXT = 512
COLS = 640
HEADS = 5
SUB = 80
SLICE = 320
QUARTER = 1280
QROWS = TOK + 16
HALF = 128
RING_START = (0, 2, 4, 6, 8, 10)
X_LAST = (False, True, False, True, False, True)
EPSILON = 1e-06
FLOOR_EPSILON = 1e-05
GUIDANCE = 3.0
BF = jnp.bfloat16
F32 = jnp.float32

GQ, GO, TQ, FQ, TO, FO = range(6)


def dot_nn(a, b):
    return lax.dot_general(a, b, (((1,), (0,)), ((), ())), preferred_element_type=F32)


def dot_nt(a, b):
    return lax.dot_general(a, b, (((1,), (1,)), ((), ())), preferred_element_type=F32)


def dot_tn(a, b):
    return lax.dot_general(a, b, (((0,), (0,)), ((), ())), preferred_element_type=F32)


class Slots:
    def __init__(self):
        self.count = 0

    def take(self, number):
        first = self.count
        self.count += number
        return first


SLOTS = Slots()
RING = SLOTS.take(6 * 16)
XCH = SLOTS.take(6 * 8)
YQG = SLOTS.take(8)
YQC = SLOTS.take(8)
YMG = SLOTS.take(8)
YMC = SLOTS.take(8)
YGM = SLOTS.take(8)
YGQ = SLOTS.take(8)
YGH = SLOTS.take(8)
YRR = SLOTS.take(8)
YPR = SLOTS.take(4)
YGN = SLOTS.take(4)
YIN = SLOTS.take(4)
YDI = SLOTS.take(4)
RSC = SLOTS.take(8 * 2 * 2)
RSX = SLOTS.take(8 * 2)
AGM = SLOTS.take(4 * 2 * 3)
BUT = SLOTS.take(5)
INN = SLOTS.take(2)
N_SEM = SLOTS.count


def kernel(
    gen_steps, critic_steps, row_order, gen_input, noise,
    w_gq, w_go, w_tq, w_to, w_fq, w_fo, tab_g, tab_t, tab_f, text_keys, text_values,
    out_p, out_g,
    W, qsg, qsc, qbuf, qA, qq, probs, mb, PP, CC, SS, XX, G, an,
    xv, nv, tg, tt, tf, kraw, keys, values, modv, sel, xT, onehot, colsT,
    send_p, send_f, pbuf, fbuf, cots, gms, gmb, gq, rsend, rrecv, isend, irecv, irow, dsend, drecv,
    ssem, rsem, lsem,
):
    g = lax.axis_index("group")
    s = lax.axis_index("seq")
    m = lax.axis_index("mp")
    z, xh = s // 2, lax.rem(s, 2)
    xl, c = m // 2, lax.rem(m, 2)
    m_core = 2 * xl + 1 - c
    m_x = 2 * (1 - xl) + c
    s_x = 2 * z + 1 - xh
    z_pair = z + 1 - 2 * lax.rem(z, 2)
    z_far = z + 2 - 4 * lax.rem(z // 2, 2)
    s_up = lax.rem(z + 1, 8) * 2 + xh
    s_down = lax.rem(z + 7, 8) * 2 + xh
    s_pair = z_pair * 2 + xh
    s_far = z_far * 2 + xh
    others = [lax.rem(g + k, GROUPS) for k in (1, 2, 3)]
    pending = []
    own_w = [w.at[pl.ds(pl.multiple_of(g * SUB, 16), SUB)] for w in (w_gq, w_go, w_tq, w_fq, w_to, w_fo)]
    sample = s // 8

    def rdma(src, dst, send, recv, **where):
        return pltpu.make_async_remote_copy(
            src_ref=src, dst_ref=dst, send_sem=ssem.at[send], recv_sem=rsem.at[recv],
            device_id=where, device_id_type=pl.DeviceIdType.MESH,
        )

    def start(copy):
        copy.start()
        pending.append(copy)

    mine_of_d = pl.ds(pl.multiple_of(m * QUARTER, 128), QUARTER)
    loads = [
        pltpu.make_async_copy(gen_input, xv, lsem.at[0]),
        pltpu.make_async_copy(tab_g, tg, lsem.at[1]),
        pltpu.make_async_copy(tab_t, tt, lsem.at[2]),
        pltpu.make_async_copy(tab_f, tf, lsem.at[3]),
        pltpu.make_async_copy(text_keys.at[0], kraw, lsem.at[4]),
        pltpu.make_async_copy(text_values.at[0], values, lsem.at[5]),
        pltpu.make_async_copy(noise.at[:, mine_of_d], nv, lsem.at[6]),
    ]

    barrier = pltpu.get_barrier_semaphore()
    peers = [{"group": o} for o in others]
    peers += [{"mp": m_core}, {"mp": m_x}, {"seq": s_x}, {"seq": s_up}, {"seq": s_down}, {"seq": s_far}]
    for peer in peers:
        pl.semaphore_signal(barrier, inc=1, device_id=peer, device_id_type=pl.DeviceIdType.MESH)
    pl.semaphore_wait(barrier, len(peers))

    def rows_of(zz, x):
        return pl.ds(pl.multiple_of((lax.rem(zz + 16, 8) * 2 + x) * SUB, 16), SUB)

    def steps_of(way, side):
        return 4 if way == side else 3

    def flows(k):
        return [(way, side) for side in ((0,) if X_LAST[k] else (0, 1)) for way in (0, 1)]

    def ring_sem(k, way, side, t):
        return RING + k * 16 + (way * 2 + side) * 4 + t

    def side_x(side):
        return xh if side == 0 else 1 - xh

    def ring_send(k, way, side, t):
        rows = rows_of(z - t if way == 0 else z + t, side_x(side))
        src = own_w[k] if t == 0 and side == 0 else W.at[k, rows]
        sem = ring_sem(k, way, side, t)
        start(rdma(src, W.at[k, rows], sem, sem, seq=s_up if way == 0 else s_down))

    def ring_wait(k, way, side, t):
        rows = rows_of(z - 1 - t if way == 0 else z + 1 + t, side_x(side))
        sem = ring_sem(k, way, side, t)
        rdma(W.at[k, rows], W.at[k, rows], sem, sem, seq=s_up).wait_recv()
        return rows

    def x_send(k, number, src, rows):
        start(rdma(src, W.at[k, rows], XCH + 8 * k + number, XCH + 8 * k + number, seq=s_x))

    def x_wait(k, number, zz):
        rows = rows_of(zz, 1 - xh)
        sem = XCH + 8 * k + number
        rdma(W.at[k, rows], W.at[k, rows], sem, sem, seq=s_x).wait_recv()

    my_rows = rows_of(z, xh)
    own_loads = [pltpu.make_async_copy(own_w[k], W.at[k, my_rows], lsem.at[7 + k]) for k in range(6)]
    for k in range(6):
        if not X_LAST[k]:
            x_send(k, 0, own_w[k], my_rows)

    state = {"tick": 0, "begun": 0}

    def ring_begin(tick):
        while state["begun"] < 6 and RING_START[state["begun"]] <= tick:
            k = state["begun"]
            for way in (0, 1):
                ring_send(k, way, 0, 0)
            if X_LAST[k]:
                x_send(k, 0, own_w[k], my_rows)
            else:
                x_wait(k, 0, z)
                for way in (0, 1):
                    ring_send(k, way, 1, 0)
            state["begun"] += 1

    def ring_to(last):
        while state["tick"] <= last:
            tick = state["tick"]
            ring_begin(tick)
            for k in range(6):
                t = tick - RING_START[k]
                for way, side in flows(k):
                    if 0 <= t < steps_of(way, side):
                        rows = ring_wait(k, way, side, t)
                        if t + 1 < steps_of(way, side):
                            ring_send(k, way, side, t + 1)
                        if X_LAST[k]:
                            x_send(k, 1 + 4 * way + t, W.at[k, rows], rows)
            state["tick"] += 1

    def have(k):
        ring_to(RING_START[k] + 3)
        own_loads[k].wait()
        if X_LAST[k]:
            x_wait(k, 0, z)
            for t in range(4):
                x_wait(k, 1 + t, z - 1 - t)
            for t in range(3):
                x_wait(k, 5 + t, z + 1 + t)

    def y_send(base, dg, src, dst, h=0):
        start(rdma(src, dst, base + 4 * h + dg, base + 4 * h + g, group=others[dg - 1]))

    def y_wait(base, source, ref, h=0):
        rdma(ref, ref, base, base + 4 * h + source, group=others[0]).wait_recv()

    def start_if(cond, copy):
        @pl.when(cond)
        def _():
            copy.start()
        guarded.append((cond, copy))

    guarded = []

    def part(h):
        return pl.ds(h * HALF, HALF)

    def q_message(ref, h):
        return ref.at[pl.ds(0, 16 + HALF)] if h == 0 else ref.at[pl.ds(16 + HALF, HALF)]

    def slice_rows(index):
        return pl.ds(pl.multiple_of(index * SLICE, 16), SLICE)

    def rs_first(r, h):
        base = RSC + 4 * r + 2 * h
        for far in (1, 0):
            x = 1 - xl if far else xl
            start(rdma(PP.at[r, h, slice_rows(2 * x + 1 - c)], CC.at[r, h, x], base + far, base + x, mp=m_core))

    def rs_core_wait(r, h, x):
        base = RSC + 4 * r + 2 * h
        rdma(CC.at[r, h, x], CC.at[r, h, x], base, base + x, mp=m_core).wait_recv()

    def rs_second(r, h):
        rs_core_wait(r, h, 1 - xl)
        far = PP[r, h, slice_rows(2 * (1 - xl) + c), :].astype(F32)
        SS[r, h] = (far + CC[r, h, 1 - xl].astype(F32)).astype(BF)
        start(rdma(SS.at[r, h], XX.at[r, h], RSX + 2 * r + h, RSX + 2 * r + h, mp=m_x))

    def rs_total(r, h):
        rs_core_wait(r, h, xl)
        rdma(XX.at[r, h], XX.at[r, h], RSX + 2 * r + h, RSX + 2 * r + h, mp=m_x).wait_recv()
        return (PP[r, h, slice_rows(m), :].astype(F32) + CC[r, h, xl].astype(F32)) + XX[r, h].astype(F32)

    def ag_copy(r, h, extra, index, where):
        rows = slice_rows(index)
        sem = AGM + 6 * r + 3 * h + extra
        return rdma(G.at[r, h, rows], G.at[r, h, rows], sem, sem, mp=where)

    def ag_first(r, h):
        start(ag_copy(r, h, 0, m, m_x))
        start(ag_copy(r, h, 1, m, m_core))

    def ag_second(r, h):
        ag_copy(r, h, 0, m_x, m_x).wait_recv()
        start(ag_copy(r, h, 2, m_x, m_core))

    def ag_wait(r, h):
        ag_copy(r, h, 1, m_core, m_core).wait_recv()
        ag_copy(r, h, 2, 2 * (1 - xl) + 1 - c, m_core).wait_recv()

    def planes(r, k, ref, h):
        for i in range(4):
            rows = pl.ds(i * SLICE, SLICE)
            PP[r, h, rows, :] = dot_nt(W[k, rows, :], ref[part(h), :]).astype(BF)

    scaling = HEAD ** -0.5

    def attend(r, own, h):
        tokens = part(h)
        rows = pl.ds(16 + h * HALF, HALF)
        parts = [own] + [qbuf.at[o] for o in others]
        total = sum(p[rows, :].astype(F32) for p in parts)
        bias = sum(p[0:16, :].astype(F32) for p in parts)[0:1, :]
        qA[tokens, :] = total
        qq[tokens, :] = r * total + bias
        for n in range(HEADS):
            lanes = pl.ds(n * HEAD, HEAD)
            qh = qq[tokens, lanes]
            rq = lax.rsqrt(jnp.mean(qh * qh, axis=1, keepdims=True) + EPSILON)
            e = jnp.exp(dot_nt((qh * rq).astype(BF), keys[:, lanes]) * scaling)
            p = (e * (1.0 / jnp.sum(e, axis=1, keepdims=True))).astype(BF)
            probs[n, tokens, :] = p
            mb[g, tokens, lanes] = dot_nn(p, values[:, lanes]).astype(BF)

    def to_bf_rows(ref, value, bias, h):
        ref[pl.ds(16 + h * HALF, HALF), :] = value.astype(BF)
        if h == 0:
            ref[0:16, :] = jnp.broadcast_to(bias, (16, COLS)).astype(BF)

    ring_begin(0)
    for copy in loads + own_loads:
        copy.start()
    row = lax.broadcasted_iota(jnp.int32, (2 * SUB, 2 * SLICE), 0)
    col = lax.broadcasted_iota(jnp.int32, (2 * SUB, 2 * SLICE), 1)
    base = row + jnp.where(row >= SUB, SLICE - SUB, 0)
    for o in range(4):
        sel[o] = (col == base + o * SUB).astype(BF)
    ring_to(0)
    order = lax.broadcasted_iota(jnp.int32, (TOK, TOK), 0)
    onehot[...] = (order == row_order[...]).astype(BF)
    for copy in loads:
        copy.wait()
    picked = []
    pr = lax.broadcasted_iota(jnp.int32, (16, 16), 0)
    pc = lax.broadcasted_iota(jnp.int32, (16, 16), 1)
    for n, (tab, step) in enumerate(((tg, gen_steps), (tt, critic_steps), (tf, critic_steps))):
        for j in range(3):
            hit = jnp.where(pr == 3 * n + j, (pc == step[sample]).astype(F32), 0.0).astype(BF)
            picked.append(dot_nn(hit, tab[j]))
    modv[...] = sum(picked).astype(BF)
    ring_to(1)
    own_sel = sel[g]
    square_row = jnp.zeros((8, TOK), F32)
    square_col = jnp.zeros((TOK, 128), F32)
    for w in range(8):
        window = pl.ds(w * 2 * SLICE, 2 * SLICE)
        rows = pl.ds(w * 2 * SUB, 2 * SUB)
        piece = xv[:, window]
        xw = dot_nt(own_sel, piece)
        cw = dot_nt(own_sel, modv[:, window])
        colsT[rows, :] = cw
        xT[rows, :] = xw.astype(BF)
        axw = (xw * (1.0 + cw[:, 1:2])).astype(BF)
        for h in (0, 1):
            an[0, h, rows, :] = axw[:, h * HALF:(h + 1) * HALF]
        sq = piece.astype(F32)
        sq = (sq * sq).astype(BF)
        square_row = square_row + dot_nt(jnp.ones((8, 2 * SLICE), BF), sq)
        square_col = square_col + dot_nn(sq, jnp.ones((2 * SLICE, 128), BF))
        if w == 3:
            ring_to(2)
    r1_row = lax.rsqrt(square_row[0:1, :] * (1.0 / D) + EPSILON)
    r1 = lax.rsqrt(square_col[:, 0:1] * (1.0 / D) + EPSILON)
    for n in range(HEADS):
        lanes = pl.ds(n * HEAD, HEAD)
        kf = kraw[:, lanes].astype(F32)
        keys[:, lanes] = (kf * lax.rsqrt(jnp.mean(kf * kf, axis=1, keepdims=True) + EPSILON)).astype(BF)
    cols_b = colsT[...].astype(BF)
    mine = slice_rows(m)
    scols = colsT[mine, :]
    gate_g, gate_t, gate_f = scols[:, 2:3], scols[:, 5:6], scols[:, 8:9]
    angle = jnp.full((8, 128), critic_steps[sample] + 1).astype(F32) * (0.5 * 3.141592653589793 / (tg.shape[1] + 1.0))
    alpha, sigma = jnp.cos(angle)[0:1, 0:1], jnp.sin(angle)[0:1, 0:1]

    have(GQ)
    bias = dot_tn(cols_b, W[GQ])[0:1]
    for h in (0, 1):
        to_bf_rows(qsg, dot_tn(an[0, h], W[GQ]), bias, h)
        start_if(g != 0, rdma(q_message(qsg, h), q_message(qbuf.at[g], h), YQG + 4 * h, YQG + 4 * h + g, group=0))
    ring_to(RING_START[GO] + 3)

    gen_m = []
    for h in (0, 1):
        for k in (2, 1, 3):
            gen_m.append(rdma(mb.at[0, part(h)], mb.at[0, part(h)], YMG + 4 * h + k, YMG + 4 * h, group=others[k - 1]))

    @pl.when(g == 0)
    def _():
        for h in (0, 1):
            for o in others:
                y_wait(YQG, o, q_message(qbuf.at[o], h), h)
            attend(r1[h * HALF:(h + 1) * HALF], qsg, h)
            for copy in gen_m[3 * h:3 * h + 3]:
                copy.start()

    guarded.extend((g == 0, copy) for copy in gen_m)
    have(GO)
    ring_to(RING_START[TQ] + 3)
    for h in (0, 1):
        @pl.when(g != 0)
        def _():
            y_wait(YMG, 0, mb.at[0, part(h)], h)
        planes(0, GO, mb.at[0], h)
        rs_first(0, h)
    for h in (0, 1):
        rs_second(0, h)
    ring_to(RING_START[FQ] + 3)
    for h in (0, 1):
        total = rs_total(0, h)
        send_p[0, h] = (xT[mine, part(h)].astype(F32) + gate_g * total).astype(BF)
    nzs = jnp.concatenate([dot_nt(own_sel, nv[:, pl.ds(w * 2 * SLICE, 2 * SLICE)]) for w in (0, 1)], axis=0)
    arrs = []
    for h in (0, 1):
        arr = sum(dot_nn(send_p[0, i], onehot[part(i), part(h)]) for i in (0, 1))
        arrs.append(arr)
        G[0, h, mine, :] = (alpha * arr + sigma * nzs[:, h * HALF:(h + 1) * HALF]).astype(BF)
        ag_first(0, h)
    for h in (0, 1):
        ag_second(0, h)
    have(TQ)
    have(FQ)
    biases = (dot_tn(cols_b, W[TQ])[3:4], dot_tn(cols_b, W[FQ])[6:7])

    for h in (0, 1):
        ag_wait(0, h)
        nf = G[0, h].astype(F32)
        rsend[h] = dot_nn(jnp.ones((8, QUARTER), BF), (nf * nf).astype(BF))
        for k in (2, 1, 3):
            y_send(YRR, k, rsend.at[h], rrecv.at[g, h], h)
        an[0, h] = (nf * (1.0 + colsT[:, 4:5])).astype(BF)
        an[1, h] = (nf * (1.0 + colsT[:, 7:8])).astype(BF)
        for n, k in ((0, TQ), (1, FQ)):
            to_bf_rows(qsc.at[n], dot_tn(an[n, h], W[k]), biases[n], h)
        for k in (2, 1, 3):
            t = others[k - 1]
            start_if(t != 0, rdma(q_message(qsc.at[t // 3], h), q_message(qbuf.at[g], h),
                                  YQC + 4 * h + k, YQC + 4 * h + g, group=t))
    start_if(g != 0, rdma(send_p.at[0], pbuf.at[g], YGN, YGN + g, group=0))
    have(TO)
    rn_rows = []
    for h in (0, 1):
        square = rsend[h]
        for o in others:
            y_wait(YRR, o, rrecv.at[o, h], h)
            square = square + rrecv[o, h]
        rn_rows.append(lax.rsqrt(square[0:1, :] * (1.0 / D) + EPSILON))
        crit_m = [rdma(mb.at[g, part(h)], mb.at[g, part(h)], YMC + 4 * h + k, YMC + 4 * h + g, group=others[k - 1])
                  for k in (2, 1, 3)]

        @pl.when(g != 0)
        def _():
            for o in others:
                y_wait(YQC, o, q_message(qbuf.at[o], h), h)
            r = jnp.transpose(jnp.broadcast_to(rn_rows[h], (128, HALF)))[:, 0:1]
            attend(r, qsc.at[g // 3], h)
            for copy in crit_m:
                copy.start()

        guarded.extend((g != 0, copy) for copy in crit_m)
    have(FO)
    for h in (0, 1):
        for r in (1, 2, 3):
            @pl.when(g != r)
            def _():
                y_wait(YMC, r, mb.at[r, part(h)], h)
            planes(r, TO if r < 3 else FO, mb.at[r], h)
            rs_first(r, h)
        for r in (1, 2, 3):
            rs_second(r, h)

    dist = jnp.zeros((1, HALF), F32)
    for h in (0, 1):
        own_n = G[0, h, mine, :].astype(F32)
        preds = []
        for r in (1, 2, 3):
            gate = gate_t if r < 3 else gate_f
            send_p[r, h] = (own_n + gate * rs_total(r, h)).astype(BF)
            preds.append(send_p[r, h].astype(F32))
        cond, uncond, faked = preds
        real = GUIDANCE * cond - (GUIDANCE - 1.0) * uncond
        score = faked - real
        fake_cot = faked - arrs[h]
        G[2, h, mine, :] = (gate_t * score).astype(BF)
        ag_first(2, h)
        G[3, h, mine, :] = (gate_f * fake_cot).astype(BF)
        ag_first(3, h)
        cots[1, h] = score
        cots[2, h] = fake_cot
        dist = dist + jnp.sum(jnp.abs(arrs[h] - real), axis=0, keepdims=True)
    for h in (0, 1):
        gen_cot = sum(dot_nt(cots[1, i].astype(BF), onehot[part(h), part(i)]) for i in (0, 1))
        cots[0, h] = gen_cot
        G[1, h, mine, :] = (gate_g * gen_cot).astype(BF)
        ag_first(1, h)
    dsend[0] = jnp.broadcast_to(dist, (8, 128))

    def butterfly(step):
        where = [dict(mp=m_core), dict(mp=m_x), dict(seq=s_x), dict(seq=s_pair), dict(seq=s_far)][step]
        return rdma(dsend.at[step], drecv.at[step], BUT + step, BUT + step, **where)

    def butterfly_end(step):
        rdma(drecv.at[step], drecv.at[step], BUT + step, BUT + step, mp=m_core).wait_recv()
        dsend[step + 1] = dsend[step] + drecv[step]

    start(butterfly(0))
    for h in (0, 1):
        for r in (2, 3):
            ag_second(r, h)
    for h in (0, 1):
        for r, k in ((2, TO), (3, FO)):
            ag_wait(r, h)
            gms[r - 1, part(h), :] = dot_tn(G[r, h], W[k]).astype(BF)
        for k in (2, 1, 3):
            t = others[k - 1]
            start_if(t != 0, rdma(gms.at[(t + 1) // 2, part(h)], gmb.at[g, part(h)],
                                  YGM + 4 * h + k, YGM + 4 * h + g, group=t))
        ag_second(1, h)
    for h in (0, 1):
        ag_wait(1, h)
        gms[0, part(h), :] = dot_tn(G[1, h], W[GO]).astype(BF)
        start_if(g != 0, rdma(gms.at[0, part(h)], gmb.at[g, part(h)], YGM + 4 * h, YGM + 4 * h + g, group=0))
    for k in (2, 1, 3):
        t = others[k - 1]
        start_if(t != 0, rdma(send_p.at[t], pbuf.at[g], YPR + k, YPR + g, group=t))
    butterfly_end(0)
    start(butterfly(1))

    factor = jnp.where(g == 1, -GUIDANCE, jnp.where(g == 2, GUIDANCE - 1.0, 1.0)).astype(F32)
    for h in (0, 1):
        tokens = part(h)
        for o in others:
            y_wait(YGM, o, gmb.at[o, tokens], h)
        total = gms[(g + 1) // 2, tokens, :].astype(F32)
        for o in others:
            total = total + gmb[o, tokens, :].astype(F32)
        gmb[g, tokens, :] = (total * factor).astype(BF)
        inner = jnp.zeros((HALF, 1), F32)
        for n in range(HEADS):
            lanes = pl.ds(n * HEAD, HEAD)
            qh = qq[tokens, lanes]
            rq = lax.rsqrt(jnp.mean(qh * qh, axis=1, keepdims=True) + EPSILON)
            unit = qh * rq
            w = probs[n, tokens, :].astype(F32)
            dp = dot_nt(gmb[g, tokens, lanes], values[:, lanes])
            gs = (w * (dp - jnp.sum(w * dp, axis=1, keepdims=True))).astype(BF)
            dqn = dot_nn(gs, keys[:, lanes]) * scaling
            grad = rq * (dqn - unit * jnp.mean(unit * dqn, axis=1, keepdims=True))
            gq[g, tokens, lanes] = grad.astype(BF)
            inner = inner + jnp.sum(grad * qA[tokens, lanes], axis=1, keepdims=True)
        for k in (2, 1, 3):
            y_send(YGQ, k, gq.at[g, tokens], gq.at[g, tokens], h)
        isend[0, :, part(h)] = jnp.transpose(jnp.broadcast_to(inner, (HALF, 128)))[0:8, :]
    start(rdma(isend.at[0], irecv.at[0], INN, INN, mp=m_core))
    butterfly_end(1)
    start(butterfly(2))

    def back_planes(r, h):
        @pl.when(g != r)
        def _():
            y_wait(YGQ, r, gq.at[r, part(h)], h)
        planes(4 + r, (GQ, TQ, TQ, FQ)[r], gq.at[r], h)
        rs_first(4 + r, h)

    def inner_and_distance(stage):
        if stage == 0:
            rdma(irecv.at[0], irecv.at[0], INN, INN, mp=m_core).wait_recv()
            isend[1] = isend[0] + irecv[0]
            start(rdma(isend.at[1], irecv.at[1], INN + 1, INN + 1, mp=m_x))
            butterfly_end(2)
            start(butterfly(3))
        if stage == 1:
            rdma(irecv.at[1], irecv.at[1], INN + 1, INN + 1, mp=m_x).wait_recv()
            irow[g] = isend[1] + irecv[1]
            for k in (2, 1, 3):
                y_send(YIN, k, irow.at[g], irow.at[g])
            butterfly_end(3)
            start(butterfly(4))
        if stage == 2:
            butterfly_end(4)
            for k in (2, 1, 3):
                y_send(YDI, k, dsend.at[5], drecv.at[5 + g])

    for h in (0, 1):
        for r in (1, 2, 3):
            back_planes(r, h)
        for r in (1, 2, 3):
            rs_second(4 + r, h)
        inner_and_distance(h)
    for h in (0, 1):
        back_planes(0, h)
    for h in (0, 1):
        rs_second(4, h)
    inner_and_distance(2)
    total = dsend[5]
    for o in others:
        y_wait(YDI, o, drecv.at[5 + o])
        total = total + drecv[5 + o]
    count = float(TOK * 16 // SAMPLES * D)
    inverse = 1.0 / (jnp.sum(total[0:1, :], axis=1, keepdims=True) * (1.0 / count) + FLOOR_EPSILON)
    for o in others:
        y_wait(YIN, o, irow.at[o])
    for r in (1, 2, 3, 0):
        scale = 1.0 + scols[:, (1, 4, 4, 7)[r]:(1, 4, 4, 7)[r] + 1]
        for h in (0, 1):
            rr = r1_row[:, h * HALF:(h + 1) * HALF] if r == 0 else rn_rows[h]
            rows = xT[mine, part(h)].astype(F32) if r == 0 else G[0, h, mine, :].astype(F32)
            ct = (1.0, -GUIDANCE, GUIDANCE - 1.0, 1.0)[r] * cots[(0, 1, 1, 2)[r], h]
            cube = rr * rr * rr * (irow[r][0:1, h * HALF:(h + 1) * HALF] * (1.0 / D))
            grads = ct + rr * scale * rs_total(4 + r, h) - rows * cube
            send_f[r, h] = (grads if r == 3 else grads * inverse).astype(BF)
            start_if(g != r, rdma(send_f.at[r, h], fbuf.at[g, h], YGH + 2 * r + h, YGH + 4 * h + g, group=r))
    pbuf[g] = send_p[g]
    fbuf[g] = send_f[g]

    def assemble(buf, w, h):
        rows = pl.ds(w * 2 * SUB, 2 * SUB)
        return sum(dot_tn(buf[o, h, rows, :], sel[o]) for o in range(4))

    @pl.when(g == 0)
    def _():
        for o in others:
            y_wait(YGN, o, pbuf.at[o])

    @pl.when(g != 0)
    def _():
        for o in others:
            y_wait(YPR, o, pbuf.at[o])

    windows = [pl.ds(w * 2 * SLICE, 2 * SLICE) for w in (0, 1)]
    for h in (0, 1):
        for w in (0, 1):
            out_p[0, part(h), windows[w]] = assemble(pbuf, w, h).astype(BF)
    for h in (0, 1):
        for o in others:
            y_wait(YGH, o, fbuf.at[o, h], h)
        for w in (0, 1):
            out_g[0, part(h), windows[w]] = assemble(fbuf, w, h)

    for cond, copy in guarded:
        @pl.when(cond)
        def _():
            copy.wait_send()

    for copy in pending:
        copy.wait_send()


def on_device(*operands):
    vmem = pl.BlockSpec(memory_space=pltpu.VMEM)
    smem = pl.BlockSpec(memory_space=pltpu.SMEM)
    hbm = pl.BlockSpec(memory_space=pl.ANY)
    act = lambda *lead: pltpu.VMEM(lead + (2, SLICE, HALF), BF)
    quarter = lambda lead: pltpu.VMEM((lead, 2, QUARTER, HALF), BF)
    (gen_input, noise, gen_steps, critic_steps, row_order) = operands[:5]
    tables = [tab.transpose(1, 0, 2) for tab in operands[11:14]]
    table = pltpu.VMEM(tables[0].shape, BF)
    return pl.pallas_call(
        kernel,
        out_shape=[
            jax.ShapeDtypeStruct((1, TOK, QUARTER), BF),
            jax.ShapeDtypeStruct((1, TOK, QUARTER), F32),
        ],
        in_specs=[smem, smem, vmem] + [hbm] * 13,
        out_specs=[vmem] * 2,
        scratch_shapes=[
            pltpu.VMEM((6, QUARTER, COLS), BF),
            pltpu.VMEM((QROWS, COLS), BF),
            pltpu.VMEM((2, QROWS, COLS), BF),
            pltpu.VMEM((4, QROWS, COLS), BF),
            pltpu.VMEM((TOK, COLS), F32),
            pltpu.VMEM((TOK, COLS), F32),
            pltpu.VMEM((HEADS, TOK, TEXT), BF),
            pltpu.VMEM((4, TOK, COLS), BF),
            quarter(8),
            pltpu.VMEM((8, 2, 2, SLICE, HALF), BF),
            act(8),
            act(8),
            quarter(4),
            quarter(2),
            pltpu.VMEM((TOK, D), BF),
            pltpu.VMEM((TOK, QUARTER), BF),
            table,
            table,
            table,
            pltpu.VMEM((TEXT, COLS), BF),
            pltpu.VMEM((TEXT, COLS), BF),
            pltpu.VMEM((TEXT, COLS), BF),
            pltpu.VMEM((16, D), BF),
            pltpu.VMEM((4, 2 * SUB, 2 * SLICE), BF),
            pltpu.VMEM((QUARTER, TOK), BF),
            pltpu.VMEM((TOK, TOK), BF),
            pltpu.VMEM((QUARTER, 16), F32),
            act(4),
            act(4),
            act(4),
            act(4),
            pltpu.VMEM((3, 2, SLICE, HALF), F32),
            pltpu.VMEM((3, TOK, COLS), BF),
            pltpu.VMEM((4, TOK, COLS), BF),
            pltpu.VMEM((4, TOK, COLS), BF),
            pltpu.VMEM((2, 8, HALF), F32),
            pltpu.VMEM((4, 2, 8, HALF), F32),
            pltpu.VMEM((2, 8, TOK), F32),
            pltpu.VMEM((2, 8, TOK), F32),
            pltpu.VMEM((4, 8, TOK), F32),
            pltpu.VMEM((6, 8, 128), F32),
            pltpu.VMEM((9, 8, 128), F32),
            pltpu.SemaphoreType.DMA((N_SEM,)),
            pltpu.SemaphoreType.DMA((N_SEM,)),
            pltpu.SemaphoreType.DMA((13,)),
        ],
        compiler_params=pltpu.CompilerParams(
            collective_id=0, has_side_effects=True, vmem_limit_bytes=60 * 2**20
        ),
        cost_estimate=pl.CostEstimate(flops=8 * 10**9, bytes_accessed=10**7, transcendentals=10**6),
    )(gen_steps, critic_steps, row_order, gen_input, noise, *operands[5:11], *tables, *operands[14:])


def solution(mesh):
    placed = (
        P("seq", None),
        P("seq", None),
        P(),
        P(),
        P("seq", None),
        P("seq", "mp"),
        P("seq", "mp"),
        P("seq", "mp"),
        P("seq", "mp"),
        P("seq", "mp"),
        P("seq", "mp"),
        P(),
        P(),
        P(),
        P("group", None, "mp"),
        P("group", None, "mp"),
    )
    return jax.shard_map(
        on_device,
        mesh=mesh,
        in_specs=placed,
        out_specs=(P("group", "seq", "mp"), P("group", "seq", "mp")),
        check_vma=False,
    )
```

```python
import jax
import jax.numpy as jnp
from jax import lax
from jax.experimental import pallas as pl
from jax.experimental.pallas import tpu as pltpu
from jax.sharding import PartitionSpec as P

D = 5120
HEAD = 128
SAMPLES = 2
GROUPS = 4
TOK = 256
TEXT = 512
COLS = 640
HEADS = 5
SUB = 80
SLICE = 320
QUARTER = 1280
QROWS = TOK + 16
HALF = 128
RING_START = (0, 1, 2, 3, 4, 5)
X_LAST = (True, False, True, False, True, False)
RING_POLLS = (3, 4, 5, 5, 6)
EPSILON = 1e-06
FLOOR_EPSILON = 1e-05
GUIDANCE = 3.0
BF = jnp.bfloat16
F32 = jnp.float32

GQ, GO, TQ, FQ, TO, FO = range(6)


def dot_nn(a, b):
    return lax.dot_general(a, b, (((1,), (0,)), ((), ())), preferred_element_type=F32)


def dot_nt(a, b):
    return lax.dot_general(a, b, (((1,), (1,)), ((), ())), preferred_element_type=F32)


def dot_tn(a, b):
    return lax.dot_general(a, b, (((0,), (0,)), ((), ())), preferred_element_type=F32)


class Slots:
    def __init__(self):
        self.count = 0

    def take(self, number):
        first = self.count
        self.count += number
        return first


SLOTS = Slots()
RING = SLOTS.take(6 * 16)
XCH = SLOTS.take(6 * 8)
YQG = SLOTS.take(8)
YQC = SLOTS.take(8)
YMG = SLOTS.take(8)
YMC = SLOTS.take(8)
YGM = SLOTS.take(8)
YGQ = SLOTS.take(8)
YGH = SLOTS.take(8)
YRR = SLOTS.take(8)
YPR = SLOTS.take(4)
YGN = SLOTS.take(4)
YIN = SLOTS.take(4)
YDI = SLOTS.take(4)
RSC = SLOTS.take(8 * 2 * 2)
RSX = SLOTS.take(8 * 2)
AGM = SLOTS.take(4 * 2 * 3)
BUT = SLOTS.take(5)
INN = SLOTS.take(2)
N_SEM = SLOTS.count


def kernel(
    gen_steps, critic_steps, row_order, gen_input, noise,
    w_gq, w_go, w_tq, w_to, w_fq, w_fo, tab_g, tab_t, tab_f, text_keys, text_values,
    pbuf, fbuf,
    W, qsg, qsc, qbuf, qA, qq, probs, mb, PP, CC, SS, XX, G, an,
    xv, nv, tg, tt, tf, kraw, keys, values, xT, onehot, colsT,
    nzt, send_p, send_f, cots, gms, gmb, gq, rsend, rrecv, isend, irecv, irow, dsend, drecv,
    ssem, rsem, lsem,
):
    g = lax.axis_index("group")
    s = lax.axis_index("seq")
    m = lax.axis_index("mp")
    z, xh = s // 2, lax.rem(s, 2)
    xl, c = m // 2, lax.rem(m, 2)
    m_core = 2 * xl + 1 - c
    m_x = 2 * (1 - xl) + c
    s_x = 2 * z + 1 - xh
    z_pair = z + 1 - 2 * lax.rem(z, 2)
    z_far = z + 2 - 4 * lax.rem(z // 2, 2)
    s_up = lax.rem(z + 1, 8) * 2 + xh
    s_down = lax.rem(z + 7, 8) * 2 + xh
    s_pair = z_pair * 2 + xh
    s_far = z_far * 2 + xh
    others = [lax.rem(g + k, GROUPS) for k in (1, 2, 3)]
    pending = []
    own_w = [w.at[pl.ds(pl.multiple_of(g * SUB, 16), SUB)] for w in (w_gq, w_go, w_tq, w_fq, w_to, w_fo)]
    sample = s // 8

    def rdma(src, dst, send, recv, **where):
        return pltpu.make_async_remote_copy(
            src_ref=src, dst_ref=dst, send_sem=ssem.at[send], recv_sem=rsem.at[recv],
            device_id=where, device_id_type=pl.DeviceIdType.MESH,
        )

    def start(copy):
        copy.start()
        pending.append(copy)

    mine_of_d = pl.ds(pl.multiple_of(m * QUARTER, 128), QUARTER)
    loads = [
        pltpu.make_async_copy(gen_input, xv, lsem.at[0]),
        pltpu.make_async_copy(tab_g, tg, lsem.at[1]),
        pltpu.make_async_copy(tab_t, tt, lsem.at[2]),
        pltpu.make_async_copy(tab_f, tf, lsem.at[3]),
        pltpu.make_async_copy(text_keys.at[0], kraw, lsem.at[4]),
        pltpu.make_async_copy(text_values.at[0], values, lsem.at[5]),
        pltpu.make_async_copy(noise.at[:, mine_of_d], nv, lsem.at[6]),
    ]

    def rows_of(zz, x):
        return pl.ds(pl.multiple_of((lax.rem(zz + 16, 8) * 2 + x) * SUB, 16), SUB)

    my_rows = rows_of(z, xh)
    own_loads = [pltpu.make_async_copy(own_w[k], W.at[k, my_rows], lsem.at[7 + k]) for k in range(6)]
    for copy in loads + own_loads:
        copy.start()

    barrier = pltpu.get_barrier_semaphore()
    peers = [{"group": o} for o in others]
    peers += [{"mp": m_core}, {"mp": m_x}, {"seq": s_x}, {"seq": s_up}, {"seq": s_down}, {"seq": s_far}]
    for peer in peers:
        pl.semaphore_signal(barrier, inc=1, device_id=peer, device_id_type=pl.DeviceIdType.MESH)
    row = lax.broadcasted_iota(jnp.int32, (2 * SUB, 2 * SLICE), 0)
    col = lax.broadcasted_iota(jnp.int32, (2 * SUB, 2 * SLICE), 1)
    base = row + jnp.where(row >= SUB, SLICE - SUB, 0)
    own_sel = (col == base + g * SUB).astype(BF)
    pl.semaphore_wait(barrier, len(peers))

    def steps_of(way, side):
        return 4 if way == side else 3

    def flows(k):
        return [(way, side) for side in ((0,) if X_LAST[k] else (0, 1)) for way in (0, 1)]

    def ring_sem(k, way, side, t):
        return RING + k * 16 + (way * 2 + side) * 4 + t

    def side_x(side):
        return xh if side == 0 else 1 - xh

    def ring_send(k, way, side, t):
        rows = rows_of(z - t if way == 0 else z + t, side_x(side))
        src = own_w[k] if t == 0 and side == 0 else W.at[k, rows]
        sem = ring_sem(k, way, side, t)
        start(rdma(src, W.at[k, rows], sem, sem, seq=s_up if way == 0 else s_down))

    def ring_wait(k, way, side, t):
        rows = rows_of(z - 1 - t if way == 0 else z + 1 + t, side_x(side))
        sem = ring_sem(k, way, side, t)
        rdma(W.at[k, rows], W.at[k, rows], sem, sem, seq=s_up).wait_recv()
        return rows

    def x_send(k, number, src, rows):
        start(rdma(src, W.at[k, rows], XCH + 8 * k + number, XCH + 8 * k + number, seq=s_x))

    def x_wait(k, number, zz):
        rows = rows_of(zz, 1 - xh)
        sem = XCH + 8 * k + number
        rdma(W.at[k, rows], W.at[k, rows], sem, sem, seq=s_x).wait_recv()


    state = {"tick": 0, "begun": 0, "sent": 0}

    def x_ahead(last):
        while state["sent"] <= min(last, 5):
            if not X_LAST[state["sent"]]:
                x_send(state["sent"], 0, own_w[state["sent"]], my_rows)
            state["sent"] += 1

    def ring_begin(tick, between=None):
        while state["begun"] < 6 and RING_START[state["begun"]] <= tick:
            k = state["begun"]
            x_ahead(k)
            for way in (0, 1):
                ring_send(k, way, 0, 0)
            if X_LAST[k]:
                x_send(k, 0, own_w[k], my_rows)
            if between is not None:
                between()
            if not X_LAST[k]:
                x_wait(k, 0, z)
                for way in (0, 1):
                    ring_send(k, way, 1, 0)
            x_ahead(k + 1)
            state["begun"] += 1

    def ring_to(last):
        while state["tick"] <= last:
            tick = state["tick"]
            ring_begin(tick)
            for k in range(6):
                t = tick - RING_START[k]
                for way, side in flows(k):
                    if 0 <= t < steps_of(way, side):
                        rows = ring_wait(k, way, side, t)
                        if t + 1 < steps_of(way, side):
                            ring_send(k, way, side, t + 1)
                        if X_LAST[k]:
                            x_send(k, 1 + 4 * way + t, W.at[k, rows], rows)
            state["tick"] += 1

    def have(k):
        ring_to(RING_START[k] + 3)
        if k != GQ:
            own_loads[k].wait()
        if X_LAST[k]:
            x_wait(k, 0, z)
            for t in range(4):
                x_wait(k, 1 + t, z - 1 - t)
            for t in range(3):
                x_wait(k, 5 + t, z + 1 + t)

    def y_send(base, dg, src, dst, h=0):
        start(rdma(src, dst, base + 4 * h + dg, base + 4 * h + g, group=others[dg - 1]))

    def y_wait(base, source, ref, h=0):
        rdma(ref, ref, base, base + 4 * h + source, group=others[0]).wait_recv()

    def start_if(cond, copy):
        @pl.when(cond)
        def _():
            copy.start()
        guarded.append((cond, copy))

    guarded = []

    def part(h):
        return pl.ds(h * HALF, HALF)

    def q_message(ref, h):
        return ref.at[pl.ds(0, 16 + HALF)] if h == 0 else ref.at[pl.ds(16 + HALF, HALF)]

    def slice_rows(index):
        return pl.ds(pl.multiple_of(index * SLICE, 16), SLICE)

    def rs_first(r, h):
        base = RSC + 4 * r + 2 * h
        for far in (1, 0):
            x = 1 - xl if far else xl
            start(rdma(PP.at[r, h, slice_rows(2 * x + 1 - c)], CC.at[r, h, x], base + far, base + x, mp=m_core))

    def rs_core_wait(r, h, x):
        base = RSC + 4 * r + 2 * h
        rdma(CC.at[r, h, x], CC.at[r, h, x], base, base + x, mp=m_core).wait_recv()

    def rs_second(r, h):
        rs_core_wait(r, h, 1 - xl)
        far = PP[r, h, slice_rows(2 * (1 - xl) + c), :].astype(F32)
        SS[r, h] = (far + CC[r, h, 1 - xl].astype(F32)).astype(BF)
        start(rdma(SS.at[r, h], XX.at[r, h], RSX + 2 * r + h, RSX + 2 * r + h, mp=m_x))

    def rs_total(r, h):
        rs_core_wait(r, h, xl)
        rdma(XX.at[r, h], XX.at[r, h], RSX + 2 * r + h, RSX + 2 * r + h, mp=m_x).wait_recv()
        return (PP[r, h, slice_rows(m), :].astype(F32) + CC[r, h, xl].astype(F32)) + XX[r, h].astype(F32)

    def ag_copy(r, h, extra, index, where):
        rows = slice_rows(index)
        sem = AGM + 6 * r + 3 * h + extra
        return rdma(G.at[r, h, rows], G.at[r, h, rows], sem, sem, mp=where)

    def ag_first(r, h):
        start(ag_copy(r, h, 0, m, m_x))
        start(ag_copy(r, h, 1, m, m_core))

    def ag_second(r, h):
        ag_copy(r, h, 0, m_x, m_x).wait_recv()
        start(ag_copy(r, h, 2, m_x, m_core))

    def ag_wait(r, h):
        ag_copy(r, h, 1, m_core, m_core).wait_recv()
        ag_copy(r, h, 2, 2 * (1 - xl) + 1 - c, m_core).wait_recv()

    def planes(r, k, ref, h):
        for i in range(4):
            rows = pl.ds(i * SLICE, SLICE)
            PP[r, h, rows, :] = dot_nt(W[k, rows, :], ref[part(h), :]).astype(BF)

    scaling = HEAD ** -0.5

    def attend(r, own, h):
        tokens = part(h)
        rows = pl.ds(16 + h * HALF, HALF)
        parts = [own] + [qbuf.at[o] for o in others]
        total = sum(p[rows, :].astype(F32) for p in parts)
        bias = sum(p[0:16, :].astype(F32) for p in parts)[0:1, :]
        qA[tokens, :] = total
        qq[tokens, :] = r * total + bias
        for n in range(HEADS):
            lanes = pl.ds(n * HEAD, HEAD)
            qh = qq[tokens, lanes]
            rq = lax.rsqrt(jnp.mean(qh * qh, axis=1, keepdims=True) + EPSILON)
            e = jnp.exp(dot_nt((qh * rq).astype(BF), keys[:, lanes]) * scaling)
            p = (e * (1.0 / jnp.sum(e, axis=1, keepdims=True))).astype(BF)
            probs[n, tokens, :] = p
            mb[g, tokens, lanes] = dot_nn(p, values[:, lanes]).astype(BF)

    def to_bf_rows(ref, value, bias, h):
        ref[pl.ds(16 + h * HALF, HALF), :] = value.astype(BF)
        if h == 0:
            ref[0:16, :] = jnp.broadcast_to(bias, (16, COLS)).astype(BF)

    table_row = lax.broadcasted_iota(jnp.int32, (16, 2 * SLICE), 0)

    def prepare(w):
        window = pl.ds(w * 2 * SLICE, 2 * SLICE)
        rows = pl.ds(w * 2 * SUB, 2 * SUB)
        mods = jnp.zeros((16, 2 * SLICE), F32)
        for n, (tab, step) in enumerate(((tg, gen_steps), (tt, critic_steps), (tf, critic_steps))):
            for j in range(3):
                value = jnp.where(table_row == step[sample], tab[j, :, window].astype(F32), 0.0)
                value = jnp.sum(value, axis=0, keepdims=True)
                mods = jnp.where(table_row == 3 * n + j, value, mods)
        xw = dot_nt(own_sel, xv[:, window])
        cw = dot_nt(own_sel, mods.astype(BF))
        colsT[rows, :] = cw
        xT[rows, :] = xw.astype(BF)
        axw = (xw * (1.0 + cw[:, 1:2])).astype(BF)
        for h in (0, 1):
            an[0, h, rows, :] = axw[:, h * HALF:(h + 1) * HALF]

    def prepare_first():
        for copy in loads[:4]:
            copy.wait()
        prepare(0)
        prepare(1)

    ring_begin(0, prepare_first)
    prepare(2)
    prepare(3)
    ring_to(0)
    prepare(4)
    prepare(5)
    ring_to(1)
    prepare(6)
    prepare(7)
    own_loads[GQ].wait()
    cols_b = colsT[...].astype(BF)
    mine = slice_rows(m)
    scols = colsT[mine, :]
    gate_g, gate_t, gate_f = scols[:, 2:3], scols[:, 5:6], scols[:, 8:9]

    have(GQ)
    bias = dot_tn(cols_b, W[GQ])[0:1]
    for h in (0, 1):
        to_bf_rows(qsg, dot_tn(an[0, h], W[GQ]), bias, h)
        start_if(g != 0, rdma(q_message(qsg, h), q_message(qbuf.at[g], h), YQG + 4 * h, YQG + 4 * h + g, group=0))
    ring_to(RING_POLLS[0])
    order = lax.broadcasted_iota(jnp.int32, (TOK, TOK), 0)
    onehot[...] = (order == row_order[...]).astype(BF)
    for copy in loads[4:]:
        copy.wait()
    for n in range(HEADS):
        lanes = pl.ds(n * HEAD, HEAD)
        kf = kraw[:, lanes].astype(F32)
        keys[:, lanes] = (kf * lax.rsqrt(jnp.mean(kf * kf, axis=1, keepdims=True) + EPSILON)).astype(BF)
    square_row = jnp.zeros((8, TOK), F32)
    square_col = jnp.zeros((TOK, 128), F32)
    for w in range(8):
        sq = xv[:, pl.ds(w * 2 * SLICE, 2 * SLICE)].astype(F32)
        sq = (sq * sq).astype(BF)
        square_row = square_row + dot_nt(jnp.ones((8, 2 * SLICE), BF), sq)
        square_col = square_col + dot_nn(sq, jnp.ones((2 * SLICE, 128), BF))
    r1_row = lax.rsqrt(square_row[0:1, :] * (1.0 / D) + EPSILON)
    r1 = lax.rsqrt(square_col[:, 0:1] * (1.0 / D) + EPSILON)
    angle = jnp.full((8, 128), critic_steps[sample] + 1).astype(F32) * (0.5 * 3.141592653589793 / (tg.shape[1] + 1.0))
    alpha, sigma = jnp.cos(angle)[0:1, 0:1], jnp.sin(angle)[0:1, 0:1]
    nzs = jnp.concatenate([dot_nt(own_sel, nv[:, pl.ds(w * 2 * SLICE, 2 * SLICE)]) for w in (0, 1)], axis=0)
    nzt[...] = sigma * nzs
    ring_to(RING_POLLS[1])

    gen_m = []
    for h in (0, 1):
        for k in (2, 1, 3):
            gen_m.append(rdma(mb.at[0, part(h)], mb.at[0, part(h)], YMG + 4 * h + k, YMG + 4 * h, group=others[k - 1]))

    @pl.when(g == 0)
    def _():
        for h in (0, 1):
            for o in others:
                y_wait(YQG, o, q_message(qbuf.at[o], h), h)
            attend(r1[h * HALF:(h + 1) * HALF], qsg, h)
            for copy in gen_m[3 * h:3 * h + 3]:
                copy.start()

    guarded.extend((g == 0, copy) for copy in gen_m)
    have(GO)
    ring_to(RING_POLLS[2])
    for h in (0, 1):
        @pl.when(g != 0)
        def _():
            y_wait(YMG, 0, mb.at[0, part(h)], h)
        planes(0, GO, mb.at[0], h)
        rs_first(0, h)
    for h in (0, 1):
        rs_second(0, h)
    ring_to(RING_POLLS[3])
    for h in (0, 1):
        total = rs_total(0, h)
        send_p[0, h] = (xT[mine, part(h)].astype(F32) + gate_g * total).astype(BF)
    arrs = []
    for h in (0, 1):
        arr = sum(dot_nn(send_p[0, i], onehot[part(i), part(h)]) for i in (0, 1))
        arrs.append(arr)
        G[0, h, mine, :] = (alpha * arr + nzt[:, part(h)]).astype(BF)
        ag_first(0, h)
    for h in (0, 1):
        ag_second(0, h)
    ring_to(RING_POLLS[4])
    have(TQ)
    have(FQ)
    biases = (dot_tn(cols_b, W[TQ])[3:4], dot_tn(cols_b, W[FQ])[6:7])

    for h in (0, 1):
        ag_wait(0, h)
        nf = G[0, h].astype(F32)
        rsend[h] = dot_nn(jnp.ones((8, QUARTER), BF), (nf * nf).astype(BF))
        for k in (2, 1, 3):
            y_send(YRR, k, rsend.at[h], rrecv.at[g, h], h)
        an[0, h] = (nf * (1.0 + colsT[:, 4:5])).astype(BF)
        an[1, h] = (nf * (1.0 + colsT[:, 7:8])).astype(BF)
        for n, k in ((0, TQ), (1, FQ)):
            to_bf_rows(qsc.at[n], dot_tn(an[n, h], W[k]), biases[n], h)
        for k in (2, 1, 3):
            t = others[k - 1]
            start_if(t != 0, rdma(q_message(qsc.at[t // 3], h), q_message(qbuf.at[g], h),
                                  YQC + 4 * h + k, YQC + 4 * h + g, group=t))
    start_if(g != 0, rdma(send_p.at[0], pbuf.at[g], YGN, YGN + g, group=0))
    have(TO)
    rn_rows = []
    for h in (0, 1):
        square = rsend[h]
        for o in others:
            y_wait(YRR, o, rrecv.at[o, h], h)
            square = square + rrecv[o, h]
        rn_rows.append(lax.rsqrt(square[0:1, :] * (1.0 / D) + EPSILON))
        crit_m = [rdma(mb.at[g, part(h)], mb.at[g, part(h)], YMC + 4 * h + k, YMC + 4 * h + g, group=others[k - 1])
                  for k in (2, 1, 3)]

        @pl.when(g != 0)
        def _():
            for o in others:
                y_wait(YQC, o, q_message(qbuf.at[o], h), h)
            r = jnp.transpose(jnp.broadcast_to(rn_rows[h], (128, HALF)))[:, 0:1]
            attend(r, qsc.at[g // 3], h)
            for copy in crit_m:
                copy.start()

        guarded.extend((g != 0, copy) for copy in crit_m)
    have(FO)
    for h in (0, 1):
        for r in (1, 2, 3):
            @pl.when(g != r)
            def _():
                y_wait(YMC, r, mb.at[r, part(h)], h)
            planes(r, TO if r < 3 else FO, mb.at[r], h)
            rs_first(r, h)
        for r in (1, 2, 3):
            rs_second(r, h)

    dist = jnp.zeros((1, HALF), F32)
    for h in (0, 1):
        own_n = G[0, h, mine, :].astype(F32)
        preds = []
        for r in (1, 2, 3):
            gate = gate_t if r < 3 else gate_f
            send_p[r, h] = (own_n + gate * rs_total(r, h)).astype(BF)
            preds.append(send_p[r, h].astype(F32))
        cond, uncond, faked = preds
        real = GUIDANCE * cond - (GUIDANCE - 1.0) * uncond
        score = faked - real
        fake_cot = faked - arrs[h]
        G[2, h, mine, :] = (gate_t * score).astype(BF)
        G[3, h, mine, :] = (gate_f * fake_cot).astype(BF)
        if h == 0:
            ag_first(2, 0)
            ag_first(3, 0)
        cots[1, h] = score
        cots[2, h] = fake_cot
        dist = dist + jnp.sum(jnp.abs(arrs[h] - real), axis=0, keepdims=True)
    for h in (0, 1):
        gen_cot = sum(dot_nt(cots[1, i].astype(BF), onehot[part(h), part(i)]) for i in (0, 1))
        cots[0, h] = gen_cot
        G[1, h, mine, :] = (gate_g * gen_cot).astype(BF)
        ag_first(1, h)
    ag_first(2, 1)
    ag_first(3, 1)
    dsend[0] = jnp.broadcast_to(dist, (8, 128))

    def butterfly(step):
        where = [dict(mp=m_core), dict(mp=m_x), dict(seq=s_x), dict(seq=s_pair), dict(seq=s_far)][step]
        return rdma(dsend.at[step], drecv.at[step], BUT + step, BUT + step, **where)

    def butterfly_end(step):
        rdma(drecv.at[step], drecv.at[step], BUT + step, BUT + step, mp=m_core).wait_recv()
        dsend[step + 1] = dsend[step] + drecv[step]

    start(butterfly(0))
    def critics_back(h):
        for r, k in ((2, TO), (3, FO)):
            ag_wait(r, h)
            gms[r - 1, part(h), :] = dot_tn(G[r, h], W[k]).astype(BF)
        for k in (2, 1, 3):
            t = others[k - 1]
            start_if(t != 0, rdma(gms.at[(t + 1) // 2, part(h)], gmb.at[g, part(h)],
                                  YGM + 4 * h + k, YGM + 4 * h + g, group=t))

    for r, h in ((2, 0), (3, 0), (1, 0), (1, 1)):
        ag_second(r, h)
    critics_back(0)
    for h in (0, 1):
        ag_wait(1, h)
        gms[0, part(h), :] = dot_tn(G[1, h], W[GO]).astype(BF)
        start_if(g != 0, rdma(gms.at[0, part(h)], gmb.at[g, part(h)], YGM + 4 * h, YGM + 4 * h + g, group=0))
    for r in (2, 3):
        ag_second(r, 1)
    critics_back(1)
    butterfly_end(0)
    start(butterfly(1))

    factor = jnp.where(g == 1, -GUIDANCE, jnp.where(g == 2, GUIDANCE - 1.0, 1.0)).astype(F32)
    for h in (0, 1):
        tokens = part(h)
        for o in others:
            y_wait(YGM, o, gmb.at[o, tokens], h)
        total = gms[(g + 1) // 2, tokens, :].astype(F32)
        for o in others:
            total = total + gmb[o, tokens, :].astype(F32)
        gmb[g, tokens, :] = (total * factor).astype(BF)
        inner = jnp.zeros((HALF, 1), F32)
        for n in range(HEADS):
            lanes = pl.ds(n * HEAD, HEAD)
            qh = qq[tokens, lanes]
            rq = lax.rsqrt(jnp.mean(qh * qh, axis=1, keepdims=True) + EPSILON)
            unit = qh * rq
            w = probs[n, tokens, :].astype(F32)
            dp = dot_nt(gmb[g, tokens, lanes], values[:, lanes])
            gs = (w * (dp - jnp.sum(w * dp, axis=1, keepdims=True))).astype(BF)
            dqn = dot_nn(gs, keys[:, lanes]) * scaling
            grad = rq * (dqn - unit * jnp.mean(unit * dqn, axis=1, keepdims=True))
            gq[g, tokens, lanes] = grad.astype(BF)
            inner = inner + jnp.sum(grad * qA[tokens, lanes], axis=1, keepdims=True)
        for k in (2, 1, 3):
            y_send(YGQ, k, gq.at[g, tokens], gq.at[g, tokens], h)
        isend[0, :, part(h)] = jnp.transpose(jnp.broadcast_to(inner, (HALF, 128)))[0:8, :]
    start(rdma(isend.at[0], irecv.at[0], INN, INN, mp=m_core))
    butterfly_end(1)
    start(butterfly(2))

    def back_planes(r, h):
        @pl.when(g != r)
        def _():
            y_wait(YGQ, r, gq.at[r, part(h)], h)
        planes(4 + r, (GQ, TQ, TQ, FQ)[r], gq.at[r], h)
        rs_first(4 + r, h)

    def inner_and_distance(stage):
        if stage == 0:
            rdma(irecv.at[0], irecv.at[0], INN, INN, mp=m_core).wait_recv()
            isend[1] = isend[0] + irecv[0]
            start(rdma(isend.at[1], irecv.at[1], INN + 1, INN + 1, mp=m_x))
            butterfly_end(2)
            start(butterfly(3))
        if stage == 1:
            rdma(irecv.at[1], irecv.at[1], INN + 1, INN + 1, mp=m_x).wait_recv()
            irow[g] = isend[1] + irecv[1]
            for k in (2, 1, 3):
                y_send(YIN, k, irow.at[g], irow.at[g])
            butterfly_end(3)
            start(butterfly(4))
        if stage == 2:
            butterfly_end(4)
            for k in (2, 1, 3):
                y_send(YDI, k, dsend.at[5], drecv.at[5 + g])

    for h in (0, 1):
        for r in (1, 2, 3, 0):
            back_planes(r, h)
        for r in (1, 2, 3, 0):
            rs_second(4 + r, h)
        inner_and_distance(h)
    for k in (2, 1, 3):
        t = others[k - 1]
        start_if(t != 0, rdma(send_p.at[t], pbuf.at[g], YPR + k, YPR + g, group=t))
    inner_and_distance(2)
    total = dsend[5]
    for o in others:
        y_wait(YDI, o, drecv.at[5 + o])
        total = total + drecv[5 + o]
    count = float(TOK * 16 // SAMPLES * D)
    inverse = 1.0 / (jnp.sum(total[0:1, :], axis=1, keepdims=True) * (1.0 / count) + FLOOR_EPSILON)
    for o in others:
        y_wait(YIN, o, irow.at[o])
    for h, r in [(h, r) for h in (0, 1) for r in (1, 2, 3, 0)]:
        scale = 1.0 + scols[:, (1, 4, 4, 7)[r]:(1, 4, 4, 7)[r] + 1]
        rr = r1_row[:, h * HALF:(h + 1) * HALF] if r == 0 else rn_rows[h]
        rows = xT[mine, part(h)].astype(F32) if r == 0 else G[0, h, mine, :].astype(F32)
        ct = (1.0, -GUIDANCE, GUIDANCE - 1.0, 1.0)[r] * cots[(0, 1, 1, 2)[r], h]
        cube = rr * rr * rr * (irow[r][0:1, h * HALF:(h + 1) * HALF] * (1.0 / D))
        grads = ct + rr * scale * rs_total(4 + r, h) - rows * cube
        send_f[r, h] = (grads if r == 3 else grads * inverse).astype(BF)
        start_if(g != r, rdma(send_f.at[r, h], fbuf.at[g, h], YGH + 2 * r + h, YGH + 4 * h + g, group=r))
    pbuf[g] = send_p[g]
    fbuf[g] = send_f[g]

    @pl.when(g == 0)
    def _():
        for o in others:
            y_wait(YGN, o, pbuf.at[o])

    @pl.when(g != 0)
    def _():
        for o in others:
            y_wait(YPR, o, pbuf.at[o])

    for h in (0, 1):
        for o in others:
            y_wait(YGH, o, fbuf.at[o, h], h)

    for cond, copy in guarded:
        @pl.when(cond)
        def _():
            copy.wait_send()

    for copy in pending:
        copy.wait_send()


def assemble(p_ref, f_ref, out_p, out_g):
    row = lax.broadcasted_iota(jnp.int32, (2 * SUB, 2 * SLICE), 0)
    col = lax.broadcasted_iota(jnp.int32, (2 * SUB, 2 * SLICE), 1)
    base = row + jnp.where(row >= SUB, SLICE - SUB, 0)
    sel = [(col == base + o * SUB).astype(BF) for o in range(4)]
    out_p[0] = sum(dot_tn(p_ref[o, 0], sel[o]) for o in range(4)).astype(BF)
    out_g[0] = sum(dot_tn(f_ref[o, 0], sel[o]) for o in range(4))


def on_device(*operands):
    vmem = pl.BlockSpec(memory_space=pltpu.VMEM)
    smem = pl.BlockSpec(memory_space=pltpu.SMEM)
    hbm = pl.BlockSpec(memory_space=pl.ANY)
    act = lambda *lead: pltpu.VMEM(lead + (2, SLICE, HALF), BF)
    quarter = lambda lead: pltpu.VMEM((lead, 2, QUARTER, HALF), BF)
    (gen_input, noise, gen_steps, critic_steps, row_order) = operands[:5]
    tables = [tab.transpose(1, 0, 2) for tab in operands[11:14]]
    table = pltpu.VMEM(tables[0].shape, BF)
    predictions, grads = pl.pallas_call(
        kernel,
        out_shape=[
            jax.ShapeDtypeStruct((4, 2, SLICE, HALF), BF),
            jax.ShapeDtypeStruct((4, 2, SLICE, HALF), BF),
        ],
        in_specs=[smem, smem, vmem] + [hbm] * 13,
        out_specs=[vmem] * 2,
        scratch_shapes=[
            pltpu.VMEM((6, QUARTER, COLS), BF),
            pltpu.VMEM((QROWS, COLS), BF),
            pltpu.VMEM((2, QROWS, COLS), BF),
            pltpu.VMEM((4, QROWS, COLS), BF),
            pltpu.VMEM((TOK, COLS), F32),
            pltpu.VMEM((TOK, COLS), F32),
            pltpu.VMEM((HEADS, TOK, TEXT), BF),
            pltpu.VMEM((4, TOK, COLS), BF),
            quarter(8),
            pltpu.VMEM((8, 2, 2, SLICE, HALF), BF),
            act(8),
            act(8),
            quarter(4),
            quarter(2),
            pltpu.VMEM((TOK, D), BF),
            pltpu.VMEM((TOK, QUARTER), BF),
            table,
            table,
            table,
            pltpu.VMEM((TEXT, COLS), BF),
            pltpu.VMEM((TEXT, COLS), BF),
            pltpu.VMEM((TEXT, COLS), BF),
            pltpu.VMEM((QUARTER, TOK), BF),
            pltpu.VMEM((TOK, TOK), BF),
            pltpu.VMEM((QUARTER, 16), F32),
            pltpu.VMEM((SLICE, TOK), F32),
            act(4),
            act(4),
            pltpu.VMEM((3, 2, SLICE, HALF), F32),
            pltpu.VMEM((3, TOK, COLS), BF),
            pltpu.VMEM((4, TOK, COLS), BF),
            pltpu.VMEM((4, TOK, COLS), BF),
            pltpu.VMEM((2, 8, HALF), F32),
            pltpu.VMEM((4, 2, 8, HALF), F32),
            pltpu.VMEM((2, 8, TOK), F32),
            pltpu.VMEM((2, 8, TOK), F32),
            pltpu.VMEM((4, 8, TOK), F32),
            pltpu.VMEM((6, 8, 128), F32),
            pltpu.VMEM((9, 8, 128), F32),
            pltpu.SemaphoreType.DMA((N_SEM,)),
            pltpu.SemaphoreType.DMA((N_SEM,)),
            pltpu.SemaphoreType.DMA((13,)),
        ],
        compiler_params=pltpu.CompilerParams(
            collective_id=0, has_side_effects=True, vmem_limit_bytes=60 * 2**20
        ),
        cost_estimate=pl.CostEstimate(flops=8 * 10**9, bytes_accessed=10**7, transcendentals=10**6),
    )(gen_steps, critic_steps, row_order, gen_input, noise, *operands[5:11], *tables, *operands[14:])
    return pl.pallas_call(
        assemble,
        grid=(2, 2),
        out_shape=[
            jax.ShapeDtypeStruct((1, TOK, QUARTER), BF),
            jax.ShapeDtypeStruct((1, TOK, QUARTER), F32),
        ],
        in_specs=[pl.BlockSpec((4, 1, 2 * SUB, HALF), lambda h, w: (0, h, w, 0))] * 2,
        out_specs=[pl.BlockSpec((1, HALF, 2 * SLICE), lambda h, w: (0, h, w))] * 2,
    )(predictions, grads)


def solution(mesh):
    placed = (
        P("seq", None),
        P("seq", None),
        P(),
        P(),
        P("seq", None),
        P("seq", "mp"),
        P("seq", "mp"),
        P("seq", "mp"),
        P("seq", "mp"),
        P("seq", "mp"),
        P("seq", "mp"),
        P(),
        P(),
        P(),
        P("group", None, "mp"),
        P("group", None, "mp"),
    )
    return jax.shard_map(
        on_device,
        mesh=mesh,
        in_specs=placed,
        out_specs=(P("group", "seq", "mp"), P("group", "seq", "mp")),
        check_vma=False,
    )
```

```python
import jax
import jax.numpy as jnp
from jax import lax
from jax.experimental import pallas as pl
from jax.experimental.pallas import tpu as pltpu
from jax.sharding import PartitionSpec as P

D = 5120
HEAD = 128
SAMPLES = 2
GROUPS = 4
TOK = 256
TEXT = 512
COLS = 640
HEADS = 5
SUB = 80
SLICE = 320
QUARTER = 1280
QROWS = TOK + 16
HALF = 128
RING_START = (0, 1, 2, 3, 4, 5)
X_LAST = (True, False, True, False, True, False)
RING_POLLS = (3, 4, 5, 5, 6)
EPSILON = 1e-06
FLOOR_EPSILON = 1e-05
GUIDANCE = 3.0
BF = jnp.bfloat16
F32 = jnp.float32

GQ, GO, TQ, FQ, TO, FO = range(6)


def dot_nn(a, b):
    return lax.dot_general(a, b, (((1,), (0,)), ((), ())), preferred_element_type=F32)


def dot_nt(a, b):
    return lax.dot_general(a, b, (((1,), (1,)), ((), ())), preferred_element_type=F32)


def dot_tn(a, b):
    return lax.dot_general(a, b, (((0,), (0,)), ((), ())), preferred_element_type=F32)


class Slots:
    def __init__(self):
        self.count = 0

    def take(self, number):
        first = self.count
        self.count += number
        return first


SLOTS = Slots()
RING = SLOTS.take(6 * 16)
XCH = SLOTS.take(6 * 8)
YQG = SLOTS.take(8)
YQC = SLOTS.take(8)
YMG = SLOTS.take(8)
YMC = SLOTS.take(8)
YGM = SLOTS.take(8)
YGQ = SLOTS.take(8)
YGH = SLOTS.take(8)
YRR = SLOTS.take(8)
YPR = SLOTS.take(4)
YGN = SLOTS.take(4)
YIN = SLOTS.take(4)
YDI = SLOTS.take(4)
RSC = SLOTS.take(8 * 2 * 2)
RSX = SLOTS.take(8 * 2)
AGM = SLOTS.take(4 * 2 * 3)
BUT = SLOTS.take(5)
INN = SLOTS.take(2)
N_SEM = SLOTS.count


def kernel(
    gen_steps, critic_steps, row_order, gen_input, noise,
    w_gq, w_go, w_tq, w_to, w_fq, w_fo, tab_g, tab_t, tab_f, text_keys, text_values,
    pbuf, fbuf,
    W, qsg, qsc, qbuf, qA, qq, probs, mb, PP, CC, SS, XX, G, an,
    xv, nv, tg, tt, tf, kraw, keys, values, xT, onehot, colsT,
    nzt, send_p, send_f, cots, gms, gmb, gq, rsend, rrecv, isend, irecv, irow, dsend, drecv,
    ssem, rsem, lsem,
):
    g = lax.axis_index("group")
    s = lax.axis_index("seq")
    m = lax.axis_index("mp")
    z, xh = s // 2, lax.rem(s, 2)
    xl, c = m // 2, lax.rem(m, 2)
    m_core = 2 * xl + 1 - c
    m_x = 2 * (1 - xl) + c
    s_x = 2 * z + 1 - xh
    z_pair = z + 1 - 2 * lax.rem(z, 2)
    z_far = z + 2 - 4 * lax.rem(z // 2, 2)
    s_up = lax.rem(z + 1, 8) * 2 + xh
    s_down = lax.rem(z + 7, 8) * 2 + xh
    s_pair = z_pair * 2 + xh
    s_far = z_far * 2 + xh
    others = [lax.rem(g + k, GROUPS) for k in (1, 2, 3)]
    pending = []
    own_w = [w.at[pl.ds(pl.multiple_of(g * SUB, 16), SUB)] for w in (w_gq, w_go, w_tq, w_fq, w_to, w_fo)]
    sample = s // 8

    def rdma(src, dst, send, recv, **where):
        return pltpu.make_async_remote_copy(
            src_ref=src, dst_ref=dst, send_sem=ssem.at[send], recv_sem=rsem.at[recv],
            device_id=where, device_id_type=pl.DeviceIdType.MESH,
        )

    def start(copy):
        copy.start()
        pending.append(copy)

    mine_of_d = pl.ds(pl.multiple_of(m * QUARTER, 128), QUARTER)
    loads = [
        pltpu.make_async_copy(gen_input, xv, lsem.at[0]),
        pltpu.make_async_copy(tab_g, tg, lsem.at[1]),
        pltpu.make_async_copy(tab_t, tt, lsem.at[2]),
        pltpu.make_async_copy(tab_f, tf, lsem.at[3]),
        pltpu.make_async_copy(text_keys.at[0], kraw, lsem.at[4]),
        pltpu.make_async_copy(text_values.at[0], values, lsem.at[5]),
        pltpu.make_async_copy(noise.at[:, mine_of_d], nv, lsem.at[6]),
    ]

    def rows_of(zz, x):
        return pl.ds(pl.multiple_of((lax.rem(zz + 16, 8) * 2 + x) * SUB, 16), SUB)

    my_rows = rows_of(z, xh)
    own_loads = [pltpu.make_async_copy(own_w[k], W.at[k, my_rows], lsem.at[7 + k]) for k in range(6)]
    for copy in loads + own_loads:
        copy.start()

    barrier = pltpu.get_barrier_semaphore()
    peers = [{"group": o} for o in others]
    peers += [{"mp": m_core}, {"mp": m_x}, {"seq": s_x}, {"seq": s_up}, {"seq": s_down}, {"seq": s_far}]
    for peer in peers:
        pl.semaphore_signal(barrier, inc=1, device_id=peer, device_id_type=pl.DeviceIdType.MESH)
    row = lax.broadcasted_iota(jnp.int32, (2 * SUB, 2 * SLICE), 0)
    col = lax.broadcasted_iota(jnp.int32, (2 * SUB, 2 * SLICE), 1)
    base = row + jnp.where(row >= SUB, SLICE - SUB, 0)
    own_sel = (col == base + g * SUB).astype(BF)
    pl.semaphore_wait(barrier, len(peers))

    def steps_of(way, side):
        return 4 if way == side else 3

    def flows(k):
        return [(way, side) for side in ((0,) if X_LAST[k] else (0, 1)) for way in (0, 1)]

    def ring_sem(k, way, side, t):
        return RING + k * 16 + (way * 2 + side) * 4 + t

    def side_x(side):
        return xh if side == 0 else 1 - xh

    def ring_send(k, way, side, t):
        rows = rows_of(z - t if way == 0 else z + t, side_x(side))
        src = own_w[k] if t == 0 and side == 0 else W.at[k, rows]
        sem = ring_sem(k, way, side, t)
        start(rdma(src, W.at[k, rows], sem, sem, seq=s_up if way == 0 else s_down))

    def ring_wait(k, way, side, t):
        rows = rows_of(z - 1 - t if way == 0 else z + 1 + t, side_x(side))
        sem = ring_sem(k, way, side, t)
        rdma(W.at[k, rows], W.at[k, rows], sem, sem, seq=s_up).wait_recv()
        return rows

    def x_send(k, number, src, rows):
        start(rdma(src, W.at[k, rows], XCH + 8 * k + number, XCH + 8 * k + number, seq=s_x))

    def x_wait(k, number, zz):
        rows = rows_of(zz, 1 - xh)
        sem = XCH + 8 * k + number
        rdma(W.at[k, rows], W.at[k, rows], sem, sem, seq=s_x).wait_recv()


    state = {"tick": 0, "begun": 0, "sent": 0}

    def x_ahead(last):
        while state["sent"] <= min(last, 5):
            if not X_LAST[state["sent"]]:
                x_send(state["sent"], 0, own_w[state["sent"]], my_rows)
            state["sent"] += 1

    def ring_begin(tick, between=None):
        while state["begun"] < 6 and RING_START[state["begun"]] <= tick:
            k = state["begun"]
            x_ahead(k)
            for way in (0, 1):
                ring_send(k, way, 0, 0)
            if X_LAST[k]:
                x_send(k, 0, own_w[k], my_rows)
            if between is not None:
                between()
            if not X_LAST[k]:
                x_wait(k, 0, z)
                for way in (0, 1):
                    ring_send(k, way, 1, 0)
            x_ahead(k + 1)
            state["begun"] += 1

    def ring_to(last):
        while state["tick"] <= last:
            tick = state["tick"]
            ring_begin(tick)
            for k in range(6):
                t = tick - RING_START[k]
                for way, side in flows(k):
                    if 0 <= t < steps_of(way, side):
                        rows = ring_wait(k, way, side, t)
                        if t + 1 < steps_of(way, side):
                            ring_send(k, way, side, t + 1)
                        if X_LAST[k]:
                            x_send(k, 1 + 4 * way + t, W.at[k, rows], rows)
            state["tick"] += 1

    def have(k):
        ring_to(RING_START[k] + 3)
        if k != GQ:
            own_loads[k].wait()
        if X_LAST[k]:
            x_wait(k, 0, z)
            for t in range(4):
                x_wait(k, 1 + t, z - 1 - t)
            for t in range(3):
                x_wait(k, 5 + t, z + 1 + t)

    def y_send(base, dg, src, dst, h=0):
        start(rdma(src, dst, base + 4 * h + dg, base + 4 * h + g, group=others[dg - 1]))

    def y_wait(base, source, ref, h=0):
        rdma(ref, ref, base, base + 4 * h + source, group=others[0]).wait_recv()

    def start_if(cond, copy):
        @pl.when(cond)
        def _():
            copy.start()
        guarded.append((cond, copy))

    guarded = []

    def part(h):
        return pl.ds(h * HALF, HALF)

    def q_message(ref, h):
        return ref.at[pl.ds(0, 16 + HALF)] if h == 0 else ref.at[pl.ds(16 + HALF, HALF)]

    def slice_rows(index):
        return pl.ds(pl.multiple_of(index * SLICE, 16), SLICE)

    def rs_first(r, h):
        base = RSC + 4 * r + 2 * h
        for far in (1, 0):
            x = 1 - xl if far else xl
            start(rdma(PP.at[r, h, slice_rows(2 * x + 1 - c)], CC.at[r, h, x], base + far, base + x, mp=m_core))

    def rs_core_wait(r, h, x):
        base = RSC + 4 * r + 2 * h
        rdma(CC.at[r, h, x], CC.at[r, h, x], base, base + x, mp=m_core).wait_recv()

    def rs_second(r, h):
        rs_core_wait(r, h, 1 - xl)
        far = PP[r, h, slice_rows(2 * (1 - xl) + c), :].astype(F32)
        SS[r, h] = (far + CC[r, h, 1 - xl].astype(F32)).astype(BF)
        start(rdma(SS.at[r, h], XX.at[r, h], RSX + 2 * r + h, RSX + 2 * r + h, mp=m_x))

    def rs_total(r, h):
        rs_core_wait(r, h, xl)
        rdma(XX.at[r, h], XX.at[r, h], RSX + 2 * r + h, RSX + 2 * r + h, mp=m_x).wait_recv()
        return (PP[r, h, slice_rows(m), :].astype(F32) + CC[r, h, xl].astype(F32)) + XX[r, h].astype(F32)

    def ag_copy(r, h, extra, index, where):
        rows = slice_rows(index)
        sem = AGM + 6 * r + 3 * h + extra
        return rdma(G.at[r, h, rows], G.at[r, h, rows], sem, sem, mp=where)

    def ag_first(r, h):
        start(ag_copy(r, h, 0, m, m_x))
        start(ag_copy(r, h, 1, m, m_core))

    def ag_second(r, h):
        ag_copy(r, h, 0, m_x, m_x).wait_recv()
        start(ag_copy(r, h, 2, m_x, m_core))

    def ag_wait(r, h):
        ag_copy(r, h, 1, m_core, m_core).wait_recv()
        ag_copy(r, h, 2, 2 * (1 - xl) + 1 - c, m_core).wait_recv()

    def planes(r, k, ref, h):
        for i in range(4):
            rows = pl.ds(i * SLICE, SLICE)
            PP[r, h, rows, :] = dot_nt(W[k, rows, :], ref[part(h), :]).astype(BF)

    scaling = HEAD ** -0.5

    def attend(r, own, h):
        tokens = part(h)
        rows = pl.ds(16 + h * HALF, HALF)
        parts = [own] + [qbuf.at[o] for o in others]
        total = sum(p[rows, :].astype(F32) for p in parts)
        bias = sum(p[0:16, :].astype(F32) for p in parts)[0:1, :]
        qA[tokens, :] = total
        qq[tokens, :] = r * total + bias
        for n in range(HEADS):
            lanes = pl.ds(n * HEAD, HEAD)
            qh = qq[tokens, lanes]
            rq = lax.rsqrt(jnp.mean(qh * qh, axis=1, keepdims=True) + EPSILON)
            e = jnp.exp(dot_nt((qh * rq).astype(BF), keys[:, lanes]) * scaling)
            p = (e * (1.0 / jnp.sum(e, axis=1, keepdims=True))).astype(BF)
            probs[n, tokens, :] = p
            mb[g, tokens, lanes] = dot_nn(p, values[:, lanes]).astype(BF)

    def to_bf_rows(ref, value, bias, h):
        ref[pl.ds(16 + h * HALF, HALF), :] = value.astype(BF)
        if h == 0:
            ref[0:16, :] = jnp.broadcast_to(bias, (16, COLS)).astype(BF)

    table_row = lax.broadcasted_iota(jnp.int32, (16, 2 * SLICE), 0)

    def prepare(w):
        window = pl.ds(w * 2 * SLICE, 2 * SLICE)
        rows = pl.ds(w * 2 * SUB, 2 * SUB)
        mods = jnp.zeros((16, 2 * SLICE), F32)
        for n, (tab, step) in enumerate(((tg, gen_steps), (tt, critic_steps), (tf, critic_steps))):
            for j in range(3):
                value = jnp.where(table_row == step[sample], tab[j, :, window].astype(F32), 0.0)
                value = jnp.sum(value, axis=0, keepdims=True)
                mods = jnp.where(table_row == 3 * n + j, value, mods)
        xw = dot_nt(own_sel, xv[:, window])
        cw = dot_nt(own_sel, mods.astype(BF))
        colsT[rows, :] = cw
        xT[rows, :] = xw.astype(BF)
        axw = (xw * (1.0 + cw[:, 1:2])).astype(BF)
        for h in (0, 1):
            an[0, h, rows, :] = axw[:, h * HALF:(h + 1) * HALF]

    def prepare_first():
        for copy in loads[:4]:
            copy.wait()
        prepare(0)
        prepare(1)

    ring_begin(0, prepare_first)
    prepare(2)
    prepare(3)
    ring_to(0)
    prepare(4)
    prepare(5)
    ring_to(1)
    prepare(6)
    prepare(7)
    own_loads[GQ].wait()
    cols_b = colsT[...].astype(BF)
    mine = slice_rows(m)
    scols = colsT[mine, :]
    gate_g, gate_t, gate_f = scols[:, 2:3], scols[:, 5:6], scols[:, 8:9]

    have(GQ)
    bias = dot_tn(cols_b, W[GQ])[0:1]
    for h in (0, 1):
        to_bf_rows(qsg, dot_tn(an[0, h], W[GQ]), bias, h)
        start_if(g != 0, rdma(q_message(qsg, h), q_message(qbuf.at[g], h), YQG + 4 * h, YQG + 4 * h + g, group=0))
    ring_to(RING_POLLS[0])
    order = lax.broadcasted_iota(jnp.int32, (TOK, TOK), 0)
    onehot[...] = (order == row_order[...]).astype(BF)
    for copy in loads[4:]:
        copy.wait()
    for n in range(HEADS):
        lanes = pl.ds(n * HEAD, HEAD)
        kf = kraw[:, lanes].astype(F32)
        keys[:, lanes] = (kf * lax.rsqrt(jnp.mean(kf * kf, axis=1, keepdims=True) + EPSILON)).astype(BF)
    square_row = jnp.zeros((8, TOK), F32)
    square_col = jnp.zeros((TOK, 128), F32)
    for w in range(8):
        sq = xv[:, pl.ds(w * 2 * SLICE, 2 * SLICE)].astype(F32)
        sq = (sq * sq).astype(BF)
        square_row = square_row + dot_nt(jnp.ones((8, 2 * SLICE), BF), sq)
        square_col = square_col + dot_nn(sq, jnp.ones((2 * SLICE, 128), BF))
    r1_row = lax.rsqrt(square_row[0:1, :] * (1.0 / D) + EPSILON)
    r1 = lax.rsqrt(square_col[:, 0:1] * (1.0 / D) + EPSILON)
    angle = jnp.full((8, 128), critic_steps[sample] + 1).astype(F32) * (0.5 * 3.141592653589793 / (tg.shape[1] + 1.0))
    alpha, sigma = jnp.cos(angle)[0:1, 0:1], jnp.sin(angle)[0:1, 0:1]
    nzs = jnp.concatenate([dot_nt(own_sel, nv[:, pl.ds(w * 2 * SLICE, 2 * SLICE)]) for w in (0, 1)], axis=0)
    nzt[...] = sigma * nzs
    ring_to(RING_POLLS[1])

    gen_m = []
    for h in (0, 1):
        for k in (2, 1, 3):
            gen_m.append(rdma(mb.at[0, part(h)], mb.at[0, part(h)], YMG + 4 * h + k, YMG + 4 * h, group=others[k - 1]))

    @pl.when(g == 0)
    def _():
        for h in (0, 1):
            for o in others:
                y_wait(YQG, o, q_message(qbuf.at[o], h), h)
            attend(r1[h * HALF:(h + 1) * HALF], qsg, h)
            for copy in gen_m[3 * h:3 * h + 3]:
                copy.start()

    guarded.extend((g == 0, copy) for copy in gen_m)
    have(GO)
    ring_to(RING_POLLS[2])
    for h in (0, 1):
        @pl.when(g != 0)
        def _():
            y_wait(YMG, 0, mb.at[0, part(h)], h)
        planes(0, GO, mb.at[0], h)
        rs_first(0, h)
    for h in (0, 1):
        rs_second(0, h)
    ring_to(RING_POLLS[3])
    for h in (0, 1):
        total = rs_total(0, h)
        send_p[0, h] = (xT[mine, part(h)].astype(F32) + gate_g * total).astype(BF)
    arrs = []
    for h in (0, 1):
        arr = sum(dot_nn(send_p[0, i], onehot[part(i), part(h)]) for i in (0, 1))
        arrs.append(arr)
        G[0, h, mine, :] = (alpha * arr + nzt[:, part(h)]).astype(BF)
        ag_first(0, h)
    for h in (0, 1):
        ag_second(0, h)
    ring_to(RING_POLLS[4])
    have(TQ)
    have(FQ)
    biases = (dot_tn(cols_b, W[TQ])[3:4], dot_tn(cols_b, W[FQ])[6:7])

    for h in (0, 1):
        ag_wait(0, h)
        nf = G[0, h].astype(F32)
        rsend[h] = dot_nn(jnp.ones((8, QUARTER), BF), (nf * nf).astype(BF))
        for k in (2, 1, 3):
            y_send(YRR, k, rsend.at[h], rrecv.at[g, h], h)
        an[0, h] = (nf * (1.0 + colsT[:, 4:5])).astype(BF)
        an[1, h] = (nf * (1.0 + colsT[:, 7:8])).astype(BF)
        for n, k in ((0, TQ), (1, FQ)):
            to_bf_rows(qsc.at[n], dot_tn(an[n, h], W[k]), biases[n], h)
        for k in (2, 1, 3):
            t = others[k - 1]
            start_if(t != 0, rdma(q_message(qsc.at[t // 3], h), q_message(qbuf.at[g], h),
                                  YQC + 4 * h + k, YQC + 4 * h + g, group=t))
    start_if(g != 0, rdma(send_p.at[0], pbuf.at[g], YGN, YGN + g, group=0))
    ring_to(RING_START[TO] + 3)
    rn_rows = []
    for h in (0, 1):
        square = rsend[h]
        for o in others:
            y_wait(YRR, o, rrecv.at[o, h], h)
            square = square + rrecv[o, h]
        rn_rows.append(lax.rsqrt(square[0:1, :] * (1.0 / D) + EPSILON))
        crit_m = [rdma(mb.at[g, part(h)], mb.at[g, part(h)], YMC + 4 * h + k, YMC + 4 * h + g, group=others[k - 1])
                  for k in (2, 1, 3)]

        @pl.when(g != 0)
        def _():
            for o in others:
                y_wait(YQC, o, q_message(qbuf.at[o], h), h)
            r = jnp.transpose(jnp.broadcast_to(rn_rows[h], (128, HALF)))[:, 0:1]
            attend(r, qsc.at[g // 3], h)
            for copy in crit_m:
                copy.start()

        guarded.extend((g != 0, copy) for copy in crit_m)
    have(TO)
    have(FO)
    for h in (0, 1):
        for r in (1, 2, 3):
            @pl.when(g != r)
            def _():
                y_wait(YMC, r, mb.at[r, part(h)], h)
            planes(r, TO if r < 3 else FO, mb.at[r], h)
            rs_first(r, h)
        for r in (1, 2, 3):
            rs_second(r, h)

    dist = jnp.zeros((1, HALF), F32)
    for h in (0, 1):
        own_n = G[0, h, mine, :].astype(F32)
        preds = []
        for r in (1, 2, 3):
            gate = gate_t if r < 3 else gate_f
            send_p[r, h] = (own_n + gate * rs_total(r, h)).astype(BF)
            preds.append(send_p[r, h].astype(F32))
        cond, uncond, faked = preds
        real = GUIDANCE * cond - (GUIDANCE - 1.0) * uncond
        score = faked - real
        fake_cot = faked - arrs[h]
        G[2, h, mine, :] = (gate_t * score).astype(BF)
        G[3, h, mine, :] = (gate_f * fake_cot).astype(BF)
        if h == 0:
            ag_first(2, 0)
            ag_first(3, 0)
        cots[1, h] = score
        cots[2, h] = fake_cot
        dist = dist + jnp.sum(jnp.abs(arrs[h] - real), axis=0, keepdims=True)
    for h in (0, 1):
        gen_cot = sum(dot_nt(cots[1, i].astype(BF), onehot[part(h), part(i)]) for i in (0, 1))
        cots[0, h] = gen_cot
        G[1, h, mine, :] = (gate_g * gen_cot).astype(BF)
        ag_first(1, h)
    ag_first(2, 1)
    ag_first(3, 1)
    dsend[0] = jnp.broadcast_to(dist, (8, 128))

    def butterfly(step):
        where = [dict(mp=m_core), dict(mp=m_x), dict(seq=s_x), dict(seq=s_pair), dict(seq=s_far)][step]
        return rdma(dsend.at[step], drecv.at[step], BUT + step, BUT + step, **where)

    def butterfly_end(step):
        rdma(drecv.at[step], drecv.at[step], BUT + step, BUT + step, mp=m_core).wait_recv()
        dsend[step + 1] = dsend[step] + drecv[step]

    start(butterfly(0))
    def critics_back(h):
        for r, k in ((2, TO), (3, FO)):
            ag_wait(r, h)
            gms[r - 1, part(h), :] = dot_tn(G[r, h], W[k]).astype(BF)
        for k in (2, 1, 3):
            t = others[k - 1]
            start_if(t != 0, rdma(gms.at[(t + 1) // 2, part(h)], gmb.at[g, part(h)],
                                  YGM + 4 * h + k, YGM + 4 * h + g, group=t))

    for r, h in ((2, 0), (3, 0), (1, 0), (1, 1)):
        ag_second(r, h)
    critics_back(0)
    for h in (0, 1):
        ag_wait(1, h)
        gms[0, part(h), :] = dot_tn(G[1, h], W[GO]).astype(BF)
        start_if(g != 0, rdma(gms.at[0, part(h)], gmb.at[g, part(h)], YGM + 4 * h, YGM + 4 * h + g, group=0))
    for r in (2, 3):
        ag_second(r, 1)
    critics_back(1)
    butterfly_end(0)
    start(butterfly(1))

    factor = jnp.where(g == 1, -GUIDANCE, jnp.where(g == 2, GUIDANCE - 1.0, 1.0)).astype(F32)
    for h in (0, 1):
        tokens = part(h)
        for o in others:
            y_wait(YGM, o, gmb.at[o, tokens], h)
        total = gms[(g + 1) // 2, tokens, :].astype(F32)
        for o in others:
            total = total + gmb[o, tokens, :].astype(F32)
        gmb[g, tokens, :] = (total * factor).astype(BF)
        inner = jnp.zeros((HALF, 1), F32)
        for n in range(HEADS):
            lanes = pl.ds(n * HEAD, HEAD)
            qh = qq[tokens, lanes]
            rq = lax.rsqrt(jnp.mean(qh * qh, axis=1, keepdims=True) + EPSILON)
            unit = qh * rq
            w = probs[n, tokens, :].astype(F32)
            dp = dot_nt(gmb[g, tokens, lanes], values[:, lanes])
            gs = (w * (dp - jnp.sum(w * dp, axis=1, keepdims=True))).astype(BF)
            dqn = dot_nn(gs, keys[:, lanes]) * scaling
            grad = rq * (dqn - unit * jnp.mean(unit * dqn, axis=1, keepdims=True))
            gq[g, tokens, lanes] = grad.astype(BF)
            inner = inner + jnp.sum(grad * qA[tokens, lanes], axis=1, keepdims=True)
        for k in (2, 1, 3):
            y_send(YGQ, k, gq.at[g, tokens], gq.at[g, tokens], h)
        isend[0, :, part(h)] = jnp.transpose(jnp.broadcast_to(inner, (HALF, 128)))[0:8, :]
    start(rdma(isend.at[0], irecv.at[0], INN, INN, mp=m_core))
    butterfly_end(1)
    start(butterfly(2))

    def back_planes(r, h):
        @pl.when(g != r)
        def _():
            y_wait(YGQ, r, gq.at[r, part(h)], h)
        planes(4 + r, (GQ, TQ, TQ, FQ)[r], gq.at[r], h)
        rs_first(4 + r, h)

    def inner_and_distance(stage):
        if stage == 0:
            rdma(irecv.at[0], irecv.at[0], INN, INN, mp=m_core).wait_recv()
            isend[1] = isend[0] + irecv[0]
            start(rdma(isend.at[1], irecv.at[1], INN + 1, INN + 1, mp=m_x))
            butterfly_end(2)
            start(butterfly(3))
        if stage == 1:
            rdma(irecv.at[1], irecv.at[1], INN + 1, INN + 1, mp=m_x).wait_recv()
            irow[g] = isend[1] + irecv[1]
            for k in (2, 1, 3):
                y_send(YIN, k, irow.at[g], irow.at[g])
            butterfly_end(3)
            start(butterfly(4))
        if stage == 2:
            butterfly_end(4)
            for k in (2, 1, 3):
                y_send(YDI, k, dsend.at[5], drecv.at[5 + g])

    for h in (0, 1):
        for r in (1, 2, 3, 0):
            back_planes(r, h)
        for r in (1, 2, 3, 0):
            rs_second(4 + r, h)
        inner_and_distance(h)
    for k in (2, 1, 3):
        t = others[k - 1]
        start_if(t != 0, rdma(send_p.at[t], pbuf.at[g], YPR + k, YPR + g, group=t))
    inner_and_distance(2)
    total = dsend[5]
    for o in others:
        y_wait(YDI, o, drecv.at[5 + o])
        total = total + drecv[5 + o]
    count = float(TOK * 16 // SAMPLES * D)
    inverse = 1.0 / (jnp.sum(total[0:1, :], axis=1, keepdims=True) * (1.0 / count) + FLOOR_EPSILON)
    for o in others:
        y_wait(YIN, o, irow.at[o])
    for h, r in [(h, r) for h in (0, 1) for r in (1, 2, 3, 0)]:
        scale = 1.0 + scols[:, (1, 4, 4, 7)[r]:(1, 4, 4, 7)[r] + 1]
        rr = r1_row[:, h * HALF:(h + 1) * HALF] if r == 0 else rn_rows[h]
        rows = xT[mine, part(h)].astype(F32) if r == 0 else G[0, h, mine, :].astype(F32)
        ct = (1.0, -GUIDANCE, GUIDANCE - 1.0, 1.0)[r] * cots[(0, 1, 1, 2)[r], h]
        cube = rr * rr * rr * (irow[r][0:1, h * HALF:(h + 1) * HALF] * (1.0 / D))
        grads = ct + rr * scale * rs_total(4 + r, h) - rows * cube
        send_f[r, h] = (grads if r == 3 else grads * inverse).astype(BF)
        start_if(g != r, rdma(send_f.at[r, h], fbuf.at[g, h], YGH + 2 * r + h, YGH + 4 * h + g, group=r))
    pbuf[g] = send_p[g]
    fbuf[g] = send_f[g]

    @pl.when(g == 0)
    def _():
        for o in others:
            y_wait(YGN, o, pbuf.at[o])

    @pl.when(g != 0)
    def _():
        for o in others:
            y_wait(YPR, o, pbuf.at[o])

    for h in (0, 1):
        for o in others:
            y_wait(YGH, o, fbuf.at[o, h], h)

    for cond, copy in guarded:
        @pl.when(cond)
        def _():
            copy.wait_send()

    for copy in pending:
        copy.wait_send()


def assemble(p_ref, f_ref, out_p, out_g):
    row = lax.broadcasted_iota(jnp.int32, (2 * SUB, 2 * SLICE), 0)
    col = lax.broadcasted_iota(jnp.int32, (2 * SUB, 2 * SLICE), 1)
    base = row + jnp.where(row >= SUB, SLICE - SUB, 0)
    sel = [(col == base + o * SUB).astype(BF) for o in range(4)]
    out_p[0] = sum(dot_tn(p_ref[o, 0], sel[o]) for o in range(4)).astype(BF)
    out_g[0] = sum(dot_tn(f_ref[o, 0], sel[o]) for o in range(4))


def on_device(*operands):
    vmem = pl.BlockSpec(memory_space=pltpu.VMEM)
    smem = pl.BlockSpec(memory_space=pltpu.SMEM)
    hbm = pl.BlockSpec(memory_space=pl.ANY)
    act = lambda *lead: pltpu.VMEM(lead + (2, SLICE, HALF), BF)
    quarter = lambda lead: pltpu.VMEM((lead, 2, QUARTER, HALF), BF)
    (gen_input, noise, gen_steps, critic_steps, row_order) = operands[:5]
    tables = [tab.transpose(1, 0, 2) for tab in operands[11:14]]
    table = pltpu.VMEM(tables[0].shape, BF)
    predictions, grads = pl.pallas_call(
        kernel,
        out_shape=[
            jax.ShapeDtypeStruct((4, 2, SLICE, HALF), BF),
            jax.ShapeDtypeStruct((4, 2, SLICE, HALF), BF),
        ],
        in_specs=[smem, smem, vmem] + [hbm] * 13,
        out_specs=[vmem] * 2,
        scratch_shapes=[
            pltpu.VMEM((6, QUARTER, COLS), BF),
            pltpu.VMEM((QROWS, COLS), BF),
            pltpu.VMEM((2, QROWS, COLS), BF),
            pltpu.VMEM((4, QROWS, COLS), BF),
            pltpu.VMEM((TOK, COLS), F32),
            pltpu.VMEM((TOK, COLS), F32),
            pltpu.VMEM((HEADS, TOK, TEXT), BF),
            pltpu.VMEM((4, TOK, COLS), BF),
            quarter(8),
            pltpu.VMEM((8, 2, 2, SLICE, HALF), BF),
            act(8),
            act(8),
            quarter(4),
            quarter(2),
            pltpu.VMEM((TOK, D), BF),
            pltpu.VMEM((TOK, QUARTER), BF),
            table,
            table,
            table,
            pltpu.VMEM((TEXT, COLS), BF),
            pltpu.VMEM((TEXT, COLS), BF),
            pltpu.VMEM((TEXT, COLS), BF),
            pltpu.VMEM((QUARTER, TOK), BF),
            pltpu.VMEM((TOK, TOK), BF),
            pltpu.VMEM((QUARTER, 16), F32),
            pltpu.VMEM((SLICE, TOK), F32),
            act(4),
            act(4),
            pltpu.VMEM((3, 2, SLICE, HALF), F32),
            pltpu.VMEM((3, TOK, COLS), BF),
            pltpu.VMEM((4, TOK, COLS), BF),
            pltpu.VMEM((4, TOK, COLS), BF),
            pltpu.VMEM((2, 8, HALF), F32),
            pltpu.VMEM((4, 2, 8, HALF), F32),
            pltpu.VMEM((2, 8, TOK), F32),
            pltpu.VMEM((2, 8, TOK), F32),
            pltpu.VMEM((4, 8, TOK), F32),
            pltpu.VMEM((6, 8, 128), F32),
            pltpu.VMEM((9, 8, 128), F32),
            pltpu.SemaphoreType.DMA((N_SEM,)),
            pltpu.SemaphoreType.DMA((N_SEM,)),
            pltpu.SemaphoreType.DMA((13,)),
        ],
        compiler_params=pltpu.CompilerParams(
            collective_id=0, has_side_effects=True, vmem_limit_bytes=60 * 2**20
        ),
        cost_estimate=pl.CostEstimate(flops=8 * 10**9, bytes_accessed=10**7, transcendentals=10**6),
    )(gen_steps, critic_steps, row_order, gen_input, noise, *operands[5:11], *tables, *operands[14:])
    return pl.pallas_call(
        assemble,
        grid=(2, 2),
        out_shape=[
            jax.ShapeDtypeStruct((1, TOK, QUARTER), BF),
            jax.ShapeDtypeStruct((1, TOK, QUARTER), F32),
        ],
        in_specs=[pl.BlockSpec((4, 1, 2 * SUB, HALF), lambda h, w: (0, h, w, 0))] * 2,
        out_specs=[pl.BlockSpec((1, HALF, 2 * SLICE), lambda h, w: (0, h, w))] * 2,
    )(predictions, grads)


def solution(mesh):
    placed = (
        P("seq", None),
        P("seq", None),
        P(),
        P(),
        P("seq", None),
        P("seq", "mp"),
        P("seq", "mp"),
        P("seq", "mp"),
        P("seq", "mp"),
        P("seq", "mp"),
        P("seq", "mp"),
        P(),
        P(),
        P(),
        P("group", None, "mp"),
        P("group", None, "mp"),
    )
    return jax.shard_map(
        on_device,
        mesh=mesh,
        in_specs=placed,
        out_specs=(P("group", "seq", "mp"), P("group", "seq", "mp")),
        check_vma=False,
    )
```
